32 devices in a mesh: view: 1, slab: 32 (over z, y, x, core).
Axes of the slice: x: 2, y: 2, z: 4, core: 2. Of those that a mesh axis runs over, the one named last changes fastest.
Arguments:
- image: float32 [128, 512, 512], P('slab'), may hold values from 0.1 to 10
- sensitivity: float32 [128, 512, 512], P('slab', 'view'), may hold values from 0.5 to 4
- resample_x: bfloat16 [2, 512, 512], P('view'), may hold values from 0 to 1, as said below
- resample_y: bfloat16 [2, 512, 512], P('view'), may hold values from 0 to 1, as said below
- tof_kernel: bfloat16 [2, 16, 512], P('view'), may hold values from 0.00019454956 to 0.0078125
- axial_mix: float32 [2, 128, 128], P('view'), may hold values from 0 to 1
- background: float32 [2, 16, 512, 128], P('view', None, 'slab'), may hold values from 0.5 to 2
- counts: int32 [2, 16, 512, 128], P('view', None, 'slab'), may hold values from 0 to 19
Outputs:
- new_image: float32 [128, 512, 512], P('slab', 'view')
The draws below stay inside these ranges and needn't reach their ends.
Inputs may be any that keep to these rules, and one draw needn't show every extreme that they name: resample_x[v, a, x] is zero where |x - a| > 3. resample_y[v, y, b] is zero where |b - y| > 3.
All inputs are finite; a program needn't handle non-finite values.
Results may differ from the reference program's by a relative error of at most 0.00052.
Values may be sent and summed in bfloat16 or wider, within the bound.
No kernel may reach another device: no remote copies, remote signals or barrier semaphores. Data moves between devices by JAX's collectives and lax.ppermute only.
A program may use at most 64 MiB of HBM per device.

```python
import math
import jax
import jax.numpy as jnp
from jax import lax

NX = 512
NY = 512
TOF_BINS = 16
BAND = 3
VIEWS = 2
SLICES = 128


def banded_blur(key, cells):
    key_shift, key_width, key_factor = jax.random.split(key, 3)
    shift = jax.random.uniform(key_shift, (VIEWS, 1, 1), jnp.float32, -0.5, 0.5)
    width = jax.random.uniform(key_width, (VIEWS, 1, 1), jnp.float32, 0.7, 1.3)
    factor = jax.random.uniform(key_factor, (VIEWS, cells, cells), jnp.float32, 0.5, 1.5)
    row_index = jnp.arange(cells, dtype=jnp.int32)[:, None]
    col_index = jnp.arange(cells, dtype=jnp.int32)[None, :]
    offset = col_index - row_index
    inside = jnp.abs(offset) <= BAND
    distance = offset.astype(jnp.float32)[None]
    profile = jnp.exp(-(distance - shift) ** 2 / (2.0 * width * width))
    values = jnp.where(inside[None], 0.4 * factor * profile, 0.0)
    return values.astype(jnp.bfloat16)


def draw_resample_x(key, part):
    return banded_blur(jax.random.fold_in(key, 11), NX)


def draw_resample_y(key, part):
    return banded_blur(jax.random.fold_in(key, 23), NY)


def draw_axial_mix(key, part):
    key_spread, key_factor = jax.random.split(jax.random.fold_in(key, 37), 2)
    spread = jnp.exp(jax.random.uniform(key_spread, (VIEWS, 1, 1), jnp.float32, 0.0, 1.0) * jnp.log(SLICES / 8.0))
    factor = jax.random.uniform(key_factor, (VIEWS, SLICES, SLICES), jnp.float32, 0.5, 1.5)
    plane_index = jnp.arange(SLICES, dtype=jnp.int32)[:, None]
    slice_index = jnp.arange(SLICES, dtype=jnp.int32)[None, :]
    distance = (plane_index - slice_index).astype(jnp.float32)[None]
    profile = jnp.exp(-(distance * distance) / (2.0 * spread * spread))
    return 0.4 / spread * factor * profile


def set_ends(values, rng, smallest, largest):
    longest = values.shape.index(max(values.shape))
    spots = []
    for shift in (0, 1):
        where = [jax.random.randint(jax.random.fold_in(rng, axis), (), 0, length) for axis, length in enumerate(values.shape)]
        where[longest] = (where[longest] + shift) % values.shape[longest]
        spots.append(tuple(where))
    return values.at[spots[0]].set(smallest).at[spots[1]].set(largest)


def block_levels(key, extent, cuts, least, top_value):
    level, own = 1.0, jax.random.fold_in(key, 6)
    for axis_at, blocks in cuts:
        heights = jnp.exp(jax.random.uniform(jax.random.fold_in(own, axis_at), (blocks,), jnp.float32, least / len(cuts), top_value / len(cuts)))
        level = level * jnp.repeat(heights, extent[axis_at] // blocks).reshape([-1 if axis == axis_at else 1 for axis in range(len(extent))])
    return level


def setup_inputs(seed: int = 0) -> dict:
    arg_keys = jax.random.split(jax.random.key(seed), 9)
    image = jnp.clip(jnp.exp(math.log(10.0) - 4.6051702 * jax.random.uniform(arg_keys[0], (SLICES, NX, NY), jnp.float32) ** block_levels(arg_keys[0], (SLICES, NX, NY), ((0, 32),), -0.2, 0.2)), 0.1, 10.0)
    sensitivity = jnp.clip(jnp.exp(math.log(4.0) - 2.0794415 * jax.random.uniform(arg_keys[1], (SLICES, NX, NY), jnp.float32) ** block_levels(arg_keys[1], (SLICES, NX, NY), ((0, 32),), -0.2, 0.2)), 0.5, 4.0)
    resample_x = draw_resample_x(jax.random.fold_in(arg_keys[8], 71), 0)
    resample_y = draw_resample_y(jax.random.fold_in(arg_keys[8], 71), 0)
    tof_kernel = jnp.clip(jnp.exp(jax.random.uniform(arg_keys[4], (VIEWS, TOF_BINS, NX), jnp.float32, math.log(0.00019454956), math.log(0.0078125))), 0.00019454956, 0.0078125).astype(jnp.bfloat16)
    axial_mix = draw_axial_mix(jax.random.fold_in(arg_keys[8], 71), 0)
    background = jnp.clip(jnp.exp(math.log(2.0) - 1.3862944 * jax.random.uniform(arg_keys[6], (VIEWS, TOF_BINS, NY, SLICES), jnp.float32) ** block_levels(arg_keys[6], (VIEWS, TOF_BINS, NY, SLICES), ((2, 32),), -0.2, 0.2)), 0.5, 2.0)
    counts = set_ends(jax.random.randint(arg_keys[7], (VIEWS, TOF_BINS, NY, SLICES), 0, 20), jax.random.fold_in(arg_keys[7], 1), 0, 19).astype(jnp.int32)
    return dict(image=image, sensitivity=sensitivity, resample_x=resample_x, resample_y=resample_y, tof_kernel=tof_kernel, axial_mix=axial_mix, background=background, counts=counts)


def one_view(image_low, resample_xv, resample_yv, tof_v, mix_v, background_v, counts_v):
    hi = lax.Precision.HIGHEST
    along_y = jnp.einsum("zxy,yb->zxb", image_low.astype(jnp.float32), resample_yv.astype(jnp.float32)).astype(jnp.bfloat16)
    rotated = jnp.einsum("zxb,ax->zba", along_y.astype(jnp.float32), resample_xv.astype(jnp.float32)).astype(jnp.bfloat16)
    integrals = jnp.einsum("ka,zba->kbz", tof_v.astype(jnp.float32), rotated.astype(jnp.float32))
    expected = background_v + jnp.einsum("kbz,cz->kbc", integrals, mix_v, precision=hi)
    ratios = counts_v.astype(jnp.float32) / expected
    back_mixed = jnp.einsum("kbc,cz->kbz", ratios, mix_v, precision=hi).astype(jnp.bfloat16)
    frames = jnp.einsum("ka,kbz->zba", tof_v.astype(jnp.float32), back_mixed.astype(jnp.float32)).astype(jnp.bfloat16)
    unrotated = jnp.einsum("zba,yb->zya", frames.astype(jnp.float32), resample_yv.astype(jnp.float32)).astype(jnp.bfloat16)
    return jnp.einsum("zya,ax->zxy", unrotated.astype(jnp.float32), resample_xv.astype(jnp.float32))


def reference(image, sensitivity, resample_x, resample_y, tof_kernel, axial_mix, background, counts):
    image_low = image.astype(jnp.bfloat16)

    def accumulate(carry, inputs):
        resample_xv, resample_yv, tof_v, mix_v, background_v, counts_v = inputs
        return carry + one_view(image_low, resample_xv, resample_yv, tof_v, mix_v, background_v, counts_v), None

    start_sum = jnp.zeros(image.shape, jnp.float32)
    gradient, unused = lax.scan(accumulate, start_sum, (resample_x, resample_y, tof_kernel, axial_mix, background, counts))
    return image * gradient / sensitivity
```

```python
import functools

import jax
import jax.numpy as jnp
from jax import lax
from jax.experimental import pallas as pl
from jax.experimental.pallas import tpu as pltpu
from jax.sharding import PartitionSpec as P

F32, BF16 = jnp.float32, jnp.bfloat16
VMEM_LIMIT = 56 * 1024 * 1024
NN = (((1,), (0,)), ((), ()))
NT = (((1,), (1,)), ((), ()))


def dot(a, b, dims=NN):
    return lax.dot_general(a, b, dims, preferred_element_type=F32)


def halves(x):
    high = x.astype(BF16)
    return high, (x - high.astype(F32)).astype(BF16)


def dot3(a, b, dims=NN):
    ah, al = halves(a)
    bh, bl = halves(b)
    return dot(ah, bh, dims) + (dot(ah, bl, dims) + dot(al, bh, dims))


def forward_kernel(views, slices, bins, image, rx, ry, tof, out, weights, partial):
    z = pl.program_id(0)
    rows = views * bins

    @pl.when(z == 0)
    def _():
        for v in range(views):
            high, low = halves(dot(tof[v], rx[v]))
            weights[v * bins : (v + 1) * bins] = high
            weights[rows + v * bins : rows + (v + 1) * bins] = low

    both = dot(weights[...], image[0].astype(BF16))
    partial[z] = both[:rows] + both[rows:]

    @pl.when(z == slices - 1)
    def _():
        per_view = []
        for v in range(views):
            mine = jnp.concatenate(
                [partial[s, v * bins : (v + 1) * bins] for s in range(slices)], axis=0
            )
            high, low = halves(mine)
            per_view.append(dot(high, ry[v]) + dot(low, ry[v]))
        joined = jnp.concatenate(
            [
                per_view[v][s * bins : (s + 1) * bins]
                for s in range(slices)
                for v in range(views)
            ],
            axis=0,
        )
        out[...] = joined.T


def swap_blocks(parts, width):
    n = len(parts)
    lane = lax.broadcasted_iota(jnp.int32, parts[0].shape, 1) // width
    step = 1
    while step < n:
        low = (lane // step) % 2 == 0
        new = list(parts)
        for i in range(n):
            if (i // step) % 2 == 0:
                a, b = parts[i], parts[i + step]
                shift = step * width
                new[i] = jnp.where(low, a, pltpu.roll(b, shift, 1))
                new[i + step] = jnp.where(
                    low, pltpu.roll(a, a.shape[1] - shift, 1), b
                )
        parts = new
        step *= 2
    return parts


def middle_kernel(views, slices, bins, owners, held, wire, mix, background, counts, out, turned, spread):
    rows = views * bins
    lanes = slices * rows
    blocks = []
    for first in range(0, held, slices):
        parts = [
            wire[pl.ds(first + i, owners, stride=held), :] for i in range(slices)
        ]
        blocks.append(jnp.concatenate(swap_blocks(parts, rows), axis=0).T)
    for v in range(views):
        turned[...] = mix[v].T
        mixed = jnp.concatenate(
            [turned[pl.ds(s, owners, stride=slices), :] for s in range(slices)], axis=0
        )
        sums = jnp.concatenate(
            [
                blocks[j // slices][
                    (j % slices) * rows + v * bins : (j % slices) * rows + (v + 1) * bins
                ]
                for j in range(held)
            ],
            axis=0,
        )
        base = v * bins * held
        added = jnp.concatenate(
            [background[pl.ds(base + j, bins, stride=held), :] for j in range(held)], axis=0
        )
        seen = jnp.concatenate(
            [counts[pl.ds(base + j, bins, stride=held), :] for j in range(held)], axis=0
        )
        ratios = seen.astype(F32) / (added + dot3(sums, mixed))
        back = dot3(mixed, ratios, NT)
        groups = held * bins // lanes
        for s in range(slices):
            for g in range(groups):
                spread[pl.ds((s * views + v) * groups + g, owners, stride=slices * views * groups), :] = back[
                    s * owners : (s + 1) * owners, g * lanes : (g + 1) * lanes
                ]
    out[...] = spread[...].astype(BF16)


def backward_kernel(views, slices, bins, owners, held, finish, *refs):
    if finish:
        wire, rxt, ry, tof, image, sensitivity, out, wide = refs
    else:
        wire, rxt, ry, tof, out, wide = refs
    z = pl.program_id(0)
    lanes = wire.shape[1]
    per_row = lanes // bins
    groups = held // per_row

    @pl.when(z == 0)
    def _():
        wide[...] = wire[...].astype(F32)

    mask = (
        lax.broadcasted_iota(jnp.int32, (per_row, lanes), 1) // bins
        == lax.broadcasted_iota(jnp.int32, (per_row, lanes), 0)
    )
    per_owner = slices * views * groups
    total = None
    for v in range(views):
        pieces = []
        for owner in range(owners):
            for g in range(groups):
                row = owner * per_owner + (z * views + v) * groups + g
                line = jnp.broadcast_to(wide[pl.ds(row, 1), :], (per_row, lanes))
                pieces.append(jnp.where(mask, line, 0.0))
        back = jnp.concatenate(pieces, axis=0).astype(BF16)
        frames = dot(back, tof[v]).astype(BF16)
        unrotated = dot(ry[v], frames).astype(BF16)
        term = dot(rxt[v], unrotated, NT)
        total = term if total is None else total + term
    if finish:
        out[0] = image[0] * total / sensitivity[0]
    else:
        out[0] = total


def local(view_size, image, sensitivity, resample_x, resample_y, tof_kernel, axial_mix, background, counts):
    views, bins, cells = tof_kernel.shape
    slices, nx, ny = image.shape
    held, planes = background.shape[2:]
    owners = planes // slices
    lanes = slices * views * bins
    params = pltpu.CompilerParams(
        dimension_semantics=("arbitrary",), vmem_limit_bytes=VMEM_LIMIT
    )
    whole = lambda x: pl.BlockSpec(x.shape, lambda z: (0,) * x.ndim)
    plane = pl.BlockSpec((1, nx, ny), lambda z: (z, 0, 0))

    rxt = jnp.swapaxes(resample_x, 1, 2)
    wire = pl.pallas_call(
        functools.partial(forward_kernel, views, slices, bins),
        grid=(slices,),
        in_specs=[plane, whole(resample_x), whole(resample_y), whole(tof_kernel)],
        out_specs=pl.BlockSpec((ny, lanes), lambda z: (0, 0)),
        out_shape=jax.ShapeDtypeStruct((ny, lanes), F32),
        scratch_shapes=[
            pltpu.VMEM((2 * views * bins, nx), BF16),
            pltpu.VMEM((slices, views * bins, ny), F32),
        ],
        compiler_params=params,
        name="project",
    )(image, resample_x, resample_y, tof_kernel)
    wire = lax.all_to_all(
        wire.reshape(owners, held, lanes), "slab", 0, 0, tiled=True
    ).reshape(ny, lanes)

    per_owner = slices * views * (held * bins // lanes)
    back = pl.pallas_call(
        functools.partial(middle_kernel, views, slices, bins, owners, held),
        out_shape=jax.ShapeDtypeStruct((owners * per_owner, lanes), BF16),
        scratch_shapes=[
            pltpu.VMEM((planes, planes), F32),
            pltpu.VMEM((owners * per_owner, lanes), F32),
        ],
        compiler_params=pltpu.CompilerParams(vmem_limit_bytes=VMEM_LIMIT),
        name="compare",
    )(
        wire,
        axial_mix,
        background.reshape(-1, planes),
        counts.reshape(-1, planes),
    )
    back = lax.all_to_all(
        back.reshape(owners, per_owner, lanes), "slab", 0, 0, tiled=True
    ).reshape(owners * per_owner, lanes)

    tiled_tof = jnp.tile(tof_kernel, (1, lanes // bins, 1))
    finish = view_size == 1
    operands = [back, rxt, resample_y, tiled_tof]
    specs = [whole(x) for x in operands]
    if finish:
        operands += [image, sensitivity]
        specs += [plane, plane]
    result = pl.pallas_call(
        functools.partial(backward_kernel, views, slices, bins, owners, held, finish),
        grid=(slices,),
        in_specs=specs,
        out_specs=plane,
        out_shape=jax.ShapeDtypeStruct((slices, nx, ny), F32),
        scratch_shapes=[pltpu.VMEM((owners * per_owner, lanes), F32)],
        compiler_params=params,
        name="backproject",
    )(*operands)
    if finish:
        return result
    gradient = lax.psum_scatter(result, "view", scatter_dimension=1, tiled=True)
    own_rows = nx // view_size
    current = lax.dynamic_slice_in_dim(image, lax.axis_index("view") * own_rows, own_rows, 1)
    return current * gradient / sensitivity


def solution(mesh):
    in_specs = (
        P("slab", None, None),
        P("slab", "view", None),
        P("view", None, None),
        P("view", None, None),
        P("view", None, None),
        P("view", None, None),
        P("view", None, "slab", None),
        P("view", None, "slab", None),
    )
    out_specs = P("slab", "view", None)
    return jax.shard_map(
        functools.partial(local, mesh.shape["view"]),
        mesh=mesh,
        in_specs=in_specs,
        out_specs=out_specs,
        check_vma=False,
    )
```

```python
import functools

import jax
import jax.numpy as jnp
from jax import lax
from jax.experimental import pallas as pl
from jax.experimental.pallas import tpu as pltpu
from jax.sharding import PartitionSpec as P

F32, BF16 = jnp.float32, jnp.bfloat16
VMEM_LIMIT = 24 * 1024 * 1024
FIRST_LIMIT = 60 * 1024 * 1024
BLOCK = 256
POWER, OFFSET = 20.75, 86.5
NN = (((1,), (0,)), ((), ()))
NT = (((1,), (1,)), ((), ()))


def dot(a, b, dims=NN):
    return lax.dot_general(a, b, dims, preferred_element_type=F32)


def halves(x):
    high = x.astype(BF16)
    return high, (x - high.astype(F32)).astype(BF16)


def dot3(a, b, dims=NN):
    ah, al = halves(a)
    bh, bl = halves(b)
    return dot(ah, bh, dims) + (dot(ah, bl, dims) + dot(al, bh, dims))


def encode(x):
    return jnp.exp(POWER * jnp.log(1.0 + 2.0 * x) - OFFSET).astype(BF16)


def decode(y):
    return 0.5 * jnp.exp((jnp.log(y.astype(F32)) + OFFSET) * (1.0 / POWER)) - 0.5


def in_hbm(x):
    return pltpu.with_memory_space_constraint(x, pltpu.HBM)


def forward_kernel(views, slices, bins, image_hbm, rx_hbm, ry_hbm, tof_hbm, out, image, rxt, ry, tof, rx, sems):
    first = pltpu.make_async_copy(tof_hbm, tof, sems.at[2 + slices])
    first.start()
    loads = [pltpu.make_async_copy(rx_hbm, rx, sems.at[0])]
    for z in range(slices):
        loads.append(pltpu.make_async_copy(image_hbm.at[z], image.at[z], sems.at[1 + z]))
    loads.append(pltpu.make_async_copy(ry_hbm, ry, sems.at[1 + slices]))
    for load in loads:
        load.start()
    rows = views * bins

    first.wait()
    loads[0].wait()
    pairs = [halves(dot(tof[v], rx[v])) for v in range(views)]
    weights = jnp.concatenate([p[0] for p in pairs] + [p[1] for p in pairs], axis=0)
    for v in range(views):
        rxt[v] = rx[v].T
    partial = []
    for z in range(slices):
        loads[1 + z].wait()
        both = dot(weights, image[z].astype(BF16))
        partial.append(both[:rows] + both[rows:])
    loads[1 + slices].wait()
    per_view = []
    for v in range(views):
        mine = jnp.concatenate([p[v * bins : (v + 1) * bins] for p in partial], axis=0)
        both = dot(jnp.concatenate(halves(mine), axis=0), ry[v])
        per_view.append(both[: slices * bins] + both[slices * bins :])
    joined = jnp.concatenate(
        [
            per_view[v][s * bins : (s + 1) * bins]
            for s in range(slices)
            for v in range(views)
        ],
        axis=0,
    )
    out[...] = encode(joined.T)


def swap_blocks(parts, width):
    n = len(parts)
    lane = lax.broadcasted_iota(jnp.int32, parts[0].shape, 1) // width
    step = 1
    while step < n:
        low = (lane // step) % 2 == 0
        new = list(parts)
        for i in range(n):
            if (i // step) % 2 == 0:
                a, b = parts[i], parts[i + step]
                shift = step * width
                new[i] = jnp.where(low, a, pltpu.roll(b, shift, 1))
                new[i + step] = jnp.where(
                    low, pltpu.roll(a, a.shape[1] - shift, 1), b
                )
        parts = new
        step *= 2
    return parts


def middle_kernel(views, slices, bins, owners, held, wire, mix, background, counts, out, turned, spread, sums_in):
    rows = views * bins
    lanes = slices * rows
    sums_in[...] = decode(wire[...])
    blocks = []
    for first in range(0, held, slices):
        parts = [
            sums_in[pl.ds(first + i, owners, stride=held), :] for i in range(slices)
        ]
        blocks.append(jnp.concatenate(swap_blocks(parts, rows), axis=0).T)
    for v in range(views):
        turned[...] = mix[v].T
        mixed = jnp.concatenate(
            [turned[pl.ds(s, owners, stride=slices), :] for s in range(slices)], axis=0
        )
        sums = jnp.concatenate(
            [
                blocks[j // slices][
                    (j % slices) * rows + v * bins : (j % slices) * rows + (v + 1) * bins
                ]
                for j in range(held)
            ],
            axis=0,
        )
        base = v * bins * held
        added = jnp.concatenate(
            [background[pl.ds(base + j, bins, stride=held), :] for j in range(held)], axis=0
        )
        seen = jnp.concatenate(
            [counts[pl.ds(base + j, bins, stride=held), :] for j in range(held)], axis=0
        )
        ratios = seen.astype(F32) / (added + dot3(sums, mixed))
        back = dot3(mixed, ratios, NT)
        groups = held * bins // lanes
        for s in range(slices):
            for g in range(groups):
                spread[pl.ds((s * views + v) * groups + g, owners, stride=slices * views * groups), :] = back[
                    s * owners : (s + 1) * owners, g * lanes : (g + 1) * lanes
                ]
    out[...] = spread[...].astype(BF16)


def corner(matrix, edge):
    near = matrix[edge - 8 : edge + 8, edge - 128 : edge + 128].astype(F32)
    row = lax.broadcasted_iota(jnp.int32, near.shape, 0) < 8
    column = lax.broadcasted_iota(jnp.int32, near.shape, 1) < 128
    return jnp.where(row != column, near, 0.0).astype(BF16)


def backward_kernel(views, slices, bins, owners, held, finish, *refs):
    if finish:
        wire, tof, ry, rxt, image, sensitivity_hbm, out_hbm = refs[:7]
    else:
        wire, tof, ry, rxt, out_hbm = refs[:5]
    result, wide, frames, unrotated, sensitivity, sems = refs[-6:]
    loads = []
    if finish:
        loads = [
            pltpu.make_async_copy(sensitivity_hbm.at[z], sensitivity.at[z], sems.at[image.shape[0] + z])
            for z in range(image.shape[0])
        ]
    for load in loads:
        load.start()
    cells = ry.shape[1]
    lanes = wire.shape[1]
    per_row = lanes // bins
    groups = held // per_row
    per_owner = slices * views * groups
    wide[...] = wire[...].astype(F32)
    mask = (
        lax.broadcasted_iota(jnp.int32, (per_row, lanes), 1) // bins
        == lax.broadcasted_iota(jnp.int32, (per_row, lanes), 0)
    )
    weights = [jnp.concatenate([tof[v]] * per_row, axis=0) for v in range(views)]
    for z in range(slices):
        for v in range(views):
            pieces = []
            for owner in range(owners):
                for g in range(groups):
                    row = owner * per_owner + (z * views + v) * groups + g
                    line = jnp.broadcast_to(wide[pl.ds(row, 1), :], (per_row, lanes))
                    pieces.append(jnp.where(mask, line, 0.0))
            back = jnp.concatenate(pieces, axis=0).astype(BF16)
            frames[z * views + v] = dot(back, weights[v]).astype(BF16)

    block = min(BLOCK, cells)
    edges = range(block, cells, block)
    ends = [[corner(ry[v], e)[:, 112:144] for e in edges] for v in range(views)]
    for i in range(slices * views):
        v = i % views
        for at in range(0, cells, block):
            own = dot(ry[v, at : at + block, at : at + block], frames[i, at : at + block, :])
            if at == 0:
                rows = [own]
            else:
                extra = dot(ends[v][at // block - 1], frames[i, at - 16 : at + 16, :])
                before, middle, after = rows[-1][:-8], rows[-1][-8:] + extra[:8], own[:8] + extra[8:]
                rows[-1] = jnp.concatenate([before, middle], axis=0)
                own = jnp.concatenate([after, own[8:]], axis=0)
                rows.append(own)
        for n, part in enumerate(rows):
            unrotated[i, n * block : (n + 1) * block, :] = part.astype(BF16)

    ends = [[corner(rxt[v], e) for e in edges] for v in range(views)]
    stores = []
    for z in range(slices):
        for at in range(0, cells, block):
            total = None
            for v in range(views):
                term = dot(
                    rxt[v, at : at + block, at : at + block],
                    unrotated[z * views + v, :, at : at + block],
                    NT,
                )
                total = term if total is None else total + term
            result[z, at : at + block, :] = total
        for n, e in enumerate(edges):
            total = None
            for v in range(views):
                term = dot(ends[v][n], unrotated[z * views + v, :, e - 128 : e + 128], NT)
                total = term if total is None else total + term
            result[z, e - 8 : e + 8, :] += total
        if finish:
            loads[z].wait()
            result[z] = image[z] * result[z] / sensitivity[z]
        store = pltpu.make_async_copy(result.at[z], out_hbm.at[z], sems.at[z])
        store.start()
        stores.append(store)
    for store in stores:
        store.wait()


def local(view_size, image, sensitivity, resample_x, resample_y, tof_kernel, axial_mix, background, counts):
    views, bins, cells = tof_kernel.shape
    slices, nx, ny = image.shape
    held, planes = background.shape[2:]
    owners = planes // slices
    lanes = slices * views * bins
    vmem = pl.BlockSpec(memory_space=pltpu.VMEM)
    anywhere = pl.BlockSpec(memory_space=pl.ANY)

    wire, current, rxt, ry, tof = pl.pallas_call(
        functools.partial(forward_kernel, views, slices, bins),
        in_specs=[anywhere] * 4,
        out_specs=[vmem] * 5,
        out_shape=[
            pltpu.VMEM((ny, lanes), BF16),
            pltpu.VMEM(image.shape, F32),
            pltpu.VMEM(resample_x.shape, BF16),
            pltpu.VMEM(resample_y.shape, BF16),
            pltpu.VMEM(tof_kernel.shape, BF16),
        ],
        scratch_shapes=[
            pltpu.VMEM(resample_x.shape, BF16),
            pltpu.SemaphoreType.DMA((3 + slices,)),
        ],
        compiler_params=pltpu.CompilerParams(vmem_limit_bytes=VMEM_LIMIT),
        name="project",
    )(*map(in_hbm, (image, resample_x, resample_y, tof_kernel)))
    wire = lax.all_to_all(
        wire.reshape(owners, held, lanes), "slab", 0, 0, tiled=True
    ).reshape(ny, lanes)

    per_owner = slices * views * (held * bins // lanes)
    back = pl.pallas_call(
        functools.partial(middle_kernel, views, slices, bins, owners, held),
        out_specs=vmem,
        out_shape=pltpu.VMEM((owners * per_owner, lanes), BF16),
        scratch_shapes=[
            pltpu.VMEM((planes, planes), F32),
            pltpu.VMEM((owners * per_owner, lanes), F32),
            pltpu.VMEM((owners * held, lanes), F32),
        ],
        compiler_params=pltpu.CompilerParams(vmem_limit_bytes=VMEM_LIMIT),
        name="compare",
    )(
        wire,
        axial_mix,
        background.reshape(-1, planes),
        counts.reshape(-1, planes),
    )
    back = lax.all_to_all(
        back.reshape(owners, per_owner, lanes), "slab", 0, 0, tiled=True
    ).reshape(owners * per_owner, lanes)

    finish = view_size == 1
    operands = [back, tof, ry, rxt]
    if finish:
        operands += [current, in_hbm(sensitivity)]
    stack = (slices * views, nx, ny)
    result = pl.pallas_call(
        functools.partial(backward_kernel, views, slices, bins, owners, held, finish),
        in_specs=[vmem] * 5 + [anywhere] if finish else [vmem] * 4,
        out_specs=anywhere,
        out_shape=jax.ShapeDtypeStruct((slices, nx, ny), F32),
        scratch_shapes=[
            pltpu.VMEM(image.shape, F32),
            pltpu.VMEM((owners * per_owner, lanes), F32),
            pltpu.VMEM(stack, BF16),
            pltpu.VMEM(stack, BF16),
            pltpu.VMEM(image.shape, F32),
            pltpu.SemaphoreType.DMA((2 * slices,)),
        ],
        compiler_params=pltpu.CompilerParams(vmem_limit_bytes=VMEM_LIMIT),
        name="backproject",
    )(*operands)
    if finish:
        return result
    gradient = lax.psum_scatter(result, "view", scatter_dimension=1, tiled=True)
    own_rows = nx // view_size
    own = lax.dynamic_slice_in_dim(image, lax.axis_index("view") * own_rows, own_rows, 1)
    return own * gradient / sensitivity


def solution(mesh):
    in_specs = (
        P("slab", None, None),
        P("slab", "view", None),
        P("view", None, None),
        P("view", None, None),
        P("view", None, None),
        P("view", None, None),
        P("view", None, "slab", None),
        P("view", None, "slab", None),
    )
    out_specs = P("slab", "view", None)
    return jax.shard_map(
        functools.partial(local, mesh.shape["view"]),
        mesh=mesh,
        in_specs=in_specs,
        out_specs=out_specs,
        check_vma=False,
    )
```

```python
import functools

import jax
import jax.numpy as jnp
from jax import lax
from jax.experimental import pallas as pl
from jax.experimental.pallas import tpu as pltpu
from jax.sharding import PartitionSpec as P

F32, BF16 = jnp.float32, jnp.bfloat16
VMEM_LIMIT = 24 * 1024 * 1024
FIRST_LIMIT = 60 * 1024 * 1024
BLOCK, BAND, NEAR = 256, 3, 16
POWER, OFFSET = 20.75, 86.5
NN = (((1,), (0,)), ((), ()))
NT = (((1,), (1,)), ((), ()))


def dot(a, b, dims=NN):
    return lax.dot_general(a, b, dims, preferred_element_type=F32)


def halves(x):
    high = x.astype(BF16)
    return high, (x - high.astype(F32)).astype(BF16)


def dot3(a, b, dims=NN):
    ah, al = halves(a)
    bh, bl = halves(b)
    return dot(ah, bh, dims) + (dot(ah, bl, dims) + dot(al, bh, dims))


def encode(x):
    return jnp.exp(POWER * jnp.log(1.0 + 2.0 * x) - OFFSET).astype(BF16)


def decode(y):
    return 0.5 * jnp.exp((jnp.log(y.astype(F32)) + OFFSET) * (1.0 / POWER)) - 0.5


def in_hbm(x):
    return pltpu.with_memory_space_constraint(x, pltpu.HBM)


def banded(rows, matrix, edge):
    cells = matrix.shape[0]
    block = min(BLOCK, cells)
    parts = [
        dot(rows[:, at : at + block], matrix[at : at + block, at : at + block])
        for at in range(0, cells, block)
    ]
    for n in range(1, len(parts)):
        at = n * block
        extra = dot(rows[:, at - NEAR : at + NEAR], corner(edge[n - 1]).astype(BF16))
        parts[n - 1] = jnp.concatenate(
            [parts[n - 1][:, : block - 128], parts[n - 1][:, block - 128 :] + extra[:, :128]], axis=1
        )
        parts[n] = jnp.concatenate([parts[n][:, :128] + extra[:, 128:], parts[n][:, 128:]], axis=1)
    return jnp.concatenate(parts, axis=1)


def forward_kernel(
    views, slices, bins, image_hbm, rx_hbm, ry_hbm, tof_hbm,
    out, image, rxt, ry, edge_y, edge_x, tof, rx, sems,
):
    cells = rx.shape[1]
    block = min(BLOCK, cells)

    def band_loads(source, target, edge, first):
        copies = []
        for at in range(0, cells, block):
            place = (slice(None), pl.ds(at, block), pl.ds(at, block))
            copies.append((source.at[place], target.at[place]))
            if at > 0:
                window = (slice(None), pl.ds(at - NEAR, 2 * NEAR), pl.ds(at - 128, 256))
                copies.append((source.at[window], edge.at[:, at // block - 1]))
        return [pltpu.make_async_copy(a, b, sems.at[first + n]) for n, (a, b) in enumerate(copies)]

    per_band = 2 * (cells // block) - 1
    load_tof = pltpu.make_async_copy(tof_hbm, tof, sems.at[0])
    load_x = band_loads(rx_hbm, rx, edge_x, 1)
    load_image = [
        pltpu.make_async_copy(image_hbm.at[z], image.at[z], sems.at[1 + 2 * per_band + z])
        for z in range(slices)
    ]
    load_y = band_loads(ry_hbm, ry, edge_y, 1 + per_band)
    for load in [load_tof] + load_x + load_image + load_y:
        load.start()
    rows = views * bins

    for load in [load_tof] + load_x:
        load.wait()
    pairs = [halves(banded(tof[v], rx.at[v], edge_x.at[v])) for v in range(views)]
    weights = jnp.concatenate([p[0] for p in pairs] + [p[1] for p in pairs], axis=0)
    for v in range(views):
        for at in range(0, cells, block):
            here = slice(at, at + block)
            rxt[v, here, here] = rx[v, here, here].T
    partial = []
    for z in range(slices):
        load_image[z].wait()
        both = dot(weights, image[z].astype(BF16))
        partial.append(both[:rows] + both[rows:])
    for load in load_y:
        load.wait()
    per_view = []
    for v in range(views):
        mine = jnp.concatenate([p[v * bins : (v + 1) * bins] for p in partial], axis=0)
        both = banded(jnp.concatenate(halves(mine), axis=0), ry.at[v], edge_y.at[v])
        per_view.append(both[: slices * bins] + both[slices * bins :])
    joined = jnp.concatenate(
        [
            per_view[v][s * bins : (s + 1) * bins]
            for s in range(slices)
            for v in range(views)
        ],
        axis=0,
    )
    out[...] = encode(joined.T)


def swap_blocks(parts, width):
    n = len(parts)
    lane = lax.broadcasted_iota(jnp.int32, parts[0].shape, 1) // width
    step = 1
    while step < n:
        low = (lane // step) % 2 == 0
        new = list(parts)
        for i in range(n):
            if (i // step) % 2 == 0:
                a, b = parts[i], parts[i + step]
                shift = step * width
                new[i] = jnp.where(low, a, pltpu.roll(b, shift, 1))
                new[i + step] = jnp.where(
                    low, pltpu.roll(a, a.shape[1] - shift, 1), b
                )
        parts = new
        step *= 2
    return parts


def middle_kernel(views, slices, bins, owners, held, wire, mix, background, counts, out, turned, spread, sums_in):
    rows = views * bins
    lanes = slices * rows
    sums_in[...] = decode(wire[...])
    blocks = []
    for first in range(0, held, slices):
        parts = [
            sums_in[pl.ds(first + i, owners, stride=held), :] for i in range(slices)
        ]
        blocks.append(jnp.concatenate(swap_blocks(parts, rows), axis=0).T)
    for v in range(views):
        turned[...] = mix[v].T
        mixed = jnp.concatenate(
            [turned[pl.ds(s, owners, stride=slices), :] for s in range(slices)], axis=0
        )
        sums = jnp.concatenate(
            [
                blocks[j // slices][
                    (j % slices) * rows + v * bins : (j % slices) * rows + (v + 1) * bins
                ]
                for j in range(held)
            ],
            axis=0,
        )
        base = v * bins * held
        added = jnp.concatenate(
            [background[pl.ds(base + j, bins, stride=held), :] for j in range(held)], axis=0
        )
        seen = jnp.concatenate(
            [counts[pl.ds(base + j, bins, stride=held), :] for j in range(held)], axis=0
        )
        ratios = seen.astype(F32) / (added + dot3(sums, mixed))
        back = dot3(mixed, ratios, NT)
        groups = held * bins // lanes
        for s in range(slices):
            for g in range(groups):
                spread[pl.ds((s * views + v) * groups + g, owners, stride=slices * views * groups), :] = back[
                    s * owners : (s + 1) * owners, g * lanes : (g + 1) * lanes
                ]
    out[...] = spread[...].astype(BF16)


def corner(window):
    window = window.astype(F32)
    row = lax.broadcasted_iota(jnp.int32, window.shape, 0) < window.shape[0] // 2
    column = lax.broadcasted_iota(jnp.int32, window.shape, 1) < window.shape[1] // 2
    return jnp.where(row != column, window, 0.0)


def corner_columns(window, width):
    near = corner(window)[NEAR - 8 : NEAR + 8]
    spread = lambda rows, n: jnp.broadcast_to(near[rows, n : n + 1], (8, width))
    return (
        [spread(slice(0, 8), 128 + n) for n in range(BAND)],
        [spread(slice(8, 16), 127 - n) for n in range(BAND)],
    )


def corner_rows(window, width):
    near = corner(window)[:, 120:136]
    flat = jnp.concatenate([near, jnp.zeros((2 * NEAR, 112), F32)], axis=1)
    turned = jnp.concatenate([flat, jnp.zeros((128 - 2 * NEAR, 128), F32)], axis=0).T
    spread = lambda rows, n: jnp.broadcast_to(turned[rows, n : n + 1], (8, width))
    return (
        [spread(slice(0, 8), NEAR + n) for n in range(BAND)],
        [spread(slice(8, 16), NEAR - 1 - n) for n in range(BAND)],
    )


def backward_kernel(views, slices, bins, owners, held, finish, *refs):
    if finish:
        wire, tof, ry, rxt, edge_y, edge_x, image, sensitivity, out_hbm = refs[:9]
    else:
        wire, tof, ry, rxt, edge_y, edge_x, out_hbm = refs[:7]
    result, wide, frames, unrotated, packed, sides, sems = refs[-7:]

    cells = ry.shape[1]
    lanes = wire.shape[1]
    per_row = lanes // bins
    groups = held // per_row
    per_owner = slices * views * groups
    wide[...] = wire[...].astype(F32)
    mask = (
        lax.broadcasted_iota(jnp.int32, (per_row, lanes), 1) // bins
        == lax.broadcasted_iota(jnp.int32, (per_row, lanes), 0)
    )
    weights = [jnp.concatenate([tof[v]] * per_row, axis=0) for v in range(views)]
    block = min(BLOCK, cells)
    edges = range(block, cells, block)
    ends_y = [[corner_columns(edge_y[v, n], cells) for n in range(len(edges))] for v in range(views)]
    ends_x = [[corner_rows(edge_x[v, n], cells) for n in range(len(edges))] for v in range(views)]
    stores = []

    def spread_frames(z):
        for v in range(views):
            pieces = []
            for owner in range(owners):
                for g in range(groups):
                    row = owner * per_owner + (z * views + v) * groups + g
                    line = jnp.broadcast_to(wide[pl.ds(row, 1), :], (per_row, lanes))
                    pieces.append(jnp.where(mask, line, 0.0))
            back = jnp.concatenate(pieces, axis=0).astype(BF16)
            frames[z * views + v] = dot(back, weights[v]).astype(BF16)

    def unrotate(z):
        for v in range(views):
            i = z * views + v
            rows = []
            for at in range(0, cells, block):
                own = dot(ry[v, at : at + block, at : at + block], frames[i, at : at + block, :])
                if at > 0:
                    above, below = ends_y[v][at // block - 1]
                    near = frames[i, at - 16 : at + 16, :].astype(F32)
                    last, first = rows[-1][-8:], own[:8]
                    for n in range(BAND):
                        last += above[n] * near[16 + n : 17 + n]
                        first += below[n] * near[15 - n : 16 - n]
                    rows[-1] = jnp.concatenate([rows[-1][:-8], last], axis=0)
                    own = jnp.concatenate([first, own[8:]], axis=0)
                rows.append(own)
            for n, part in enumerate(rows):
                here = slice(n * block, (n + 1) * block)
                part = part.astype(BF16)
                unrotated[i, here, :] = part
                for m, e in enumerate(edges):
                    left = part[:, e - 128 : e].astype(F32)
                    right = part[:, e : e + 128].astype(F32)
                    lane = lax.broadcasted_iota(jnp.int32, left.shape, 1)
                    spot = 16 * (i % (half * views))
                    around = pltpu.roll(jnp.where(lane < 64, right, left), (spot + 8) % 128, 1)
                    packed[z // half, m, here, spot : spot + 16] = around[:, spot : spot + 16]

    def finish_slice(z):
        strips = []
        for at in range(0, cells, block):
            total = None
            for v in range(views):
                term = dot(
                    rxt[v, at : at + block, at : at + block],
                    unrotated[z * views + v, :, at : at + block],
                    NT,
                )
                total = term if total is None else total + term
            if at > 0:
                last, first = strips[-1][-8:], total[:8]
                for v in range(views):
                    above, below = ends_x[v][at // block - 1]
                    own = (z % half * views + v) * 16
                    for n in range(BAND):
                        last += above[n] * sides[z // half, at // block - 1, pl.ds(own + 8 + n, 1), :]
                        first += below[n] * sides[z // half, at // block - 1, pl.ds(own + 7 - n, 1), :]
                strips[-1] = jnp.concatenate([strips[-1][:-8], last], axis=0)
                total = jnp.concatenate([first, total[8:]], axis=0)
            strips.append(total)
        for n, strip in enumerate(strips):
            rows = pl.ds(n * block, block)
            if finish:
                strip = image[z, rows, :] * strip / sensitivity[z, rows, :]
            result[z, rows, :] = strip
        store = pltpu.make_async_copy(result.at[z], out_hbm.at[z], sems.at[z])
        store.start()
        stores.append(store)

    half = 1
    for z in range(slices):
        spread_frames(z)
    for z in range(slices + 1):
        if z < slices:
            unrotate(z)
            for m in range(len(edges)):
                sides[z, m] = packed[z, m].T
        if z > 0:
            finish_slice(z - 1)
    for store in stores:
        store.wait()


def local(view_size, image, sensitivity, resample_x, resample_y, tof_kernel, axial_mix, background, counts):
    views, bins, cells = tof_kernel.shape
    slices, nx, ny = image.shape
    held, planes = background.shape[2:]
    owners = planes // slices
    lanes = slices * views * bins
    vmem = pl.BlockSpec(memory_space=pltpu.VMEM)
    anywhere = pl.BlockSpec(memory_space=pl.ANY)

    block = min(BLOCK, nx)
    edge_shape = (views, max(nx // block - 1, 1), 2 * NEAR, 256)
    wire, current, rxt, ry, edge_y, edge_x, tof = pl.pallas_call(
        functools.partial(forward_kernel, views, slices, bins),
        in_specs=[anywhere] * 4,
        out_specs=[vmem] * 7,
        out_shape=[
            pltpu.VMEM((ny, lanes), BF16),
            pltpu.VMEM(image.shape, F32),
            pltpu.VMEM(resample_x.shape, BF16),
            pltpu.VMEM(resample_y.shape, BF16),
            pltpu.VMEM(edge_shape, BF16),
            pltpu.VMEM(edge_shape, BF16),
            pltpu.VMEM(tof_kernel.shape, BF16),
        ],
        scratch_shapes=[
            pltpu.VMEM(resample_x.shape, BF16),
            pltpu.SemaphoreType.DMA((1 + 2 * (2 * (nx // block) - 1) + slices,)),
        ],
        compiler_params=pltpu.CompilerParams(vmem_limit_bytes=VMEM_LIMIT),
        name="project",
    )(*map(in_hbm, (image, resample_x, resample_y, tof_kernel)))
    wire = lax.all_to_all(
        wire.reshape(owners, held, lanes), "slab", 0, 0, tiled=True
    ).reshape(ny, lanes)

    per_owner = slices * views * (held * bins // lanes)
    back = pl.pallas_call(
        functools.partial(middle_kernel, views, slices, bins, owners, held),
        out_specs=vmem,
        out_shape=pltpu.VMEM((owners * per_owner, lanes), BF16),
        scratch_shapes=[
            pltpu.VMEM((planes, planes), F32),
            pltpu.VMEM((owners * per_owner, lanes), F32),
            pltpu.VMEM((owners * held, lanes), F32),
        ],
        compiler_params=pltpu.CompilerParams(vmem_limit_bytes=VMEM_LIMIT),
        cost_estimate=pl.CostEstimate(flops=0, bytes_accessed=40 * 1024 * 1024, transcendentals=0),
        name="compare",
    )(
        wire,
        axial_mix,
        background.reshape(-1, planes),
        counts.reshape(-1, planes),
    )
    back = lax.all_to_all(
        back.reshape(owners, per_owner, lanes), "slab", 0, 0, tiled=True
    ).reshape(owners * per_owner, lanes)

    finish = view_size == 1
    operands = [back, tof, ry, rxt, edge_y, edge_x]
    if finish:
        operands += [current, sensitivity]
    stack = (slices * views, nx, ny)
    result = pl.pallas_call(
        functools.partial(backward_kernel, views, slices, bins, owners, held, finish),
        in_specs=[vmem] * len(operands),
        out_specs=anywhere,
        out_shape=jax.ShapeDtypeStruct((slices, nx, ny), F32),
        scratch_shapes=[
            pltpu.VMEM(image.shape, F32),
            pltpu.VMEM((owners * per_owner, lanes), F32),
            pltpu.VMEM(stack, BF16),
            pltpu.VMEM(stack, BF16),
            pltpu.VMEM((slices, pl.cdiv(nx, BLOCK), ny, 16 * views), F32),
            pltpu.VMEM((slices, pl.cdiv(nx, BLOCK), 16 * views, ny), F32),
            pltpu.SemaphoreType.DMA((slices,)),
        ],
        compiler_params=pltpu.CompilerParams(vmem_limit_bytes=VMEM_LIMIT),
        name="backproject",
    )(*operands)
    if finish:
        return result
    gradient = lax.psum_scatter(result, "view", scatter_dimension=1, tiled=True)
    own_rows = nx // view_size
    own = lax.dynamic_slice_in_dim(image, lax.axis_index("view") * own_rows, own_rows, 1)
    return own * gradient / sensitivity


def solution(mesh):
    in_specs = (
        P("slab", None, None),
        P("slab", "view", None),
        P("view", None, None),
        P("view", None, None),
        P("view", None, None),
        P("view", None, None),
        P("view", None, "slab", None),
        P("view", None, "slab", None),
    )
    out_specs = P("slab", "view", None)
    return jax.shard_map(
        functools.partial(local, mesh.shape["view"]),
        mesh=mesh,
        in_specs=in_specs,
        out_specs=out_specs,
        check_vma=False,
    )
```

```python
import functools

import jax
import jax.numpy as jnp
from jax import lax
from jax.experimental import pallas as pl
from jax.experimental.pallas import tpu as pltpu
from jax.sharding import PartitionSpec as P

F32, BF16 = jnp.float32, jnp.bfloat16
VMEM_LIMIT = 24 * 1024 * 1024
FIRST_LIMIT = 60 * 1024 * 1024
BLOCK, NARROW, BAND, NEAR = 256, 128, 3, 16
POWER, OFFSET = 20.75, 86.5
NN = (((1,), (0,)), ((), ()))
NT = (((1,), (1,)), ((), ()))


def dot(a, b, dims=NN):
    return lax.dot_general(a, b, dims, preferred_element_type=F32)


def halves(x):
    high = x.astype(BF16)
    return high, (x - high.astype(F32)).astype(BF16)


def dot3(a, b, dims=NN):
    ah, al = halves(a)
    bh, bl = halves(b)
    return dot(ah, bh, dims) + (dot(ah, bl, dims) + dot(al, bh, dims))


def encode(x):
    return jnp.exp(POWER * jnp.log(1.0 + 2.0 * x) - OFFSET).astype(BF16)


def decode(y):
    return 0.5 * jnp.exp((jnp.log(y.astype(F32)) + OFFSET) * (1.0 / POWER)) - 0.5


def in_hbm(x):
    return pltpu.with_memory_space_constraint(x, pltpu.HBM)


def banded(rows, matrix, edge, between=1):
    cells = matrix.shape[0]
    block = min(BLOCK, cells)
    parts = [
        dot(rows[:, at : at + block], matrix[at : at + block, at : at + block])
        for at in range(0, cells, block)
    ]
    for n in range(1, len(parts)):
        at = n * block
        extra = dot(rows[:, at - NEAR : at + NEAR], corner(edge[n * between - 1]).astype(BF16))
        parts[n - 1] = jnp.concatenate(
            [parts[n - 1][:, : block - 128], parts[n - 1][:, block - 128 :] + extra[:, :128]], axis=1
        )
        parts[n] = jnp.concatenate([parts[n][:, :128] + extra[:, 128:], parts[n][:, 128:]], axis=1)
    return jnp.concatenate(parts, axis=1)


def forward_kernel(
    views, slices, bins, image_hbm, rx_hbm, ry_hbm, tof_hbm,
    out, image, strips_x, ryt, edge_y, edge_x, toft, tof, rx, ry, sems,
):
    cells = rx.shape[1]
    block = min(BLOCK, cells)

    def band(source, target, edge, step):
        copies = []
        for at in range(0, cells, block):
            place = (slice(None), pl.ds(at, block), pl.ds(at, block))
            copies.append((source.at[place], target.at[place]))
            if at > 0:
                window = (slice(None), pl.ds(at - NEAR, 2 * NEAR), pl.ds(at - 128, 256))
                copies.append((source.at[window], edge.at[:, at // step - 1]))
        return copies

    images = [(image_hbm.at[z], image.at[z]) for z in range(slices)]
    groups = [[(tof_hbm, tof)] + band(rx_hbm, rx, edge_x, NARROW)]
    groups += [images[:1], images[1:2], band(ry_hbm, ry, edge_y, block)]
    groups += [[pair] for pair in images[2:]]
    loads, n = [], 0
    for group in groups:
        loads.append([pltpu.make_async_copy(*pair, sems.at[n + i]) for i, pair in enumerate(group)])
        n += len(group)
    for load in sum(loads, []):
        load.start()
    loads = iter(loads)

    def arrive():
        for load in next(loads):
            load.wait()

    rows = views * bins
    per_row = toft.shape[2] // bins
    partial = []

    def add_slice(z):
        arrive()
        both = dot(weights, image[z].astype(BF16))
        partial.append(both[:rows] + both[rows:])

    arrive()
    pairs = [halves(banded(tof[v], rx.at[v], edge_x.at[v], block // NARROW)) for v in range(views)]
    weights = jnp.concatenate([p[0] for p in pairs] + [p[1] for p in pairs], axis=0)
    add_slice(0)
    for v in range(views):
        for n, at in enumerate(range(0, cells, NARROW)):
            strips_x[n, :, v * NARROW : (v + 1) * NARROW] = rx[v, at : at + NARROW, at : at + NARROW].T
            if at % block > 0:
                edge_x[v, n - 1] = rx[v, at - NEAR : at + NEAR, at - 128 : at + 128]
    add_slice(1)
    arrive()
    for v in range(views):
        toft[v] = jnp.concatenate([tof[v]] * per_row, axis=0).T
        for at in range(0, cells, block):
            here = slice(at, at + block)
            ryt[v, here, here] = ry[v, here, here].T
    for z in range(2, slices):
        add_slice(z)
    per_view = []
    for v in range(views):
        mine = jnp.concatenate([p[v * bins : (v + 1) * bins] for p in partial], axis=0)
        both = banded(jnp.concatenate(halves(mine), axis=0), ry.at[v], edge_y.at[v])
        per_view.append(both[: slices * bins] + both[slices * bins :])
    joined = jnp.concatenate(
        [
            per_view[v][s * bins : (s + 1) * bins]
            for s in range(slices)
            for v in range(views)
        ],
        axis=0,
    )
    out[...] = encode(joined.T)


def swap_blocks(parts, width):
    n = len(parts)
    lane = lax.broadcasted_iota(jnp.int32, parts[0].shape, 1) // width
    step = 1
    while step < n:
        low = (lane // step) % 2 == 0
        new = list(parts)
        for i in range(n):
            if (i // step) % 2 == 0:
                a, b = parts[i], parts[i + step]
                shift = step * width
                new[i] = jnp.where(low, a, pltpu.roll(b, shift, 1))
                new[i + step] = jnp.where(
                    low, pltpu.roll(a, a.shape[1] - shift, 1), b
                )
        parts = new
        step *= 2
    return parts


def middle_kernel(views, slices, bins, owners, held, wire, mix, background, counts, out, turned, spread, sums_in):
    rows = views * bins
    lanes = slices * rows
    sums_in[...] = decode(wire[...])
    blocks = []
    for first in range(0, held, slices):
        parts = [
            sums_in[pl.ds(first + i, owners, stride=held), :] for i in range(slices)
        ]
        blocks.append(jnp.concatenate(swap_blocks(parts, rows), axis=0).T)
    for v in range(views):
        turned[...] = mix[v].T
        mixed = jnp.concatenate(
            [turned[pl.ds(s, owners, stride=slices), :] for s in range(slices)], axis=0
        )
        sums = jnp.concatenate(
            [
                blocks[j // slices][
                    (j % slices) * rows + v * bins : (j % slices) * rows + (v + 1) * bins
                ]
                for j in range(held)
            ],
            axis=0,
        )
        base = v * bins * held
        added = jnp.concatenate(
            [background[pl.ds(base + j, bins, stride=held), :] for j in range(held)], axis=0
        )
        seen = jnp.concatenate(
            [counts[pl.ds(base + j, bins, stride=held), :] for j in range(held)], axis=0
        )
        ratios = seen.astype(F32) / (added + dot3(sums, mixed))
        back = dot3(mixed, ratios, NT)
        groups = held * bins // lanes
        for s in range(slices):
            for g in range(groups):
                spread[pl.ds((s * views + v) * groups + g, owners, stride=slices * views * groups), :] = back[
                    s * owners : (s + 1) * owners, g * lanes : (g + 1) * lanes
                ]
    out[...] = spread[...].astype(BF16)


def corner(window):
    window = window.astype(F32)
    row = lax.broadcasted_iota(jnp.int32, window.shape, 0) < window.shape[0] // 2
    column = lax.broadcasted_iota(jnp.int32, window.shape, 1) < window.shape[1] // 2
    return jnp.where(row != column, window, 0.0)


def corner_columns(window, width):
    near = corner(window)[NEAR - 8 : NEAR + 8]
    spread = lambda rows, n: jnp.broadcast_to(near[rows, n : n + 1], (8, width))
    return (
        [spread(slice(0, 8), 128 + n) for n in range(BAND)],
        [spread(slice(8, 16), 127 - n) for n in range(BAND)],
    )


def corner_rows(window, width):
    near = corner(window)[:, 120:136]
    flat = jnp.concatenate([near, jnp.zeros((2 * NEAR, 112), F32)], axis=1)
    turned = jnp.concatenate([flat, jnp.zeros((128 - 2 * NEAR, 128), F32)], axis=0).T
    spread = lambda rows, n: jnp.broadcast_to(turned[rows, n : n + 1], (8, width))
    return (
        [spread(slice(0, 8), NEAR + n) for n in range(BAND)],
        [spread(slice(8, 16), NEAR - 1 - n) for n in range(BAND)],
    )


def backward_kernel(views, slices, bins, owners, held, finish, *refs):
    wire, tof, toft, ryt, strips_x, edge_y, edge_x = refs[:7]
    if finish:
        image, sensitivity = refs[7:9]
    out_hbm, result, wide, frames, unrotated, turned, sems = refs[-7:]

    cells = ryt.shape[1]
    lanes = wire.shape[1]
    per_row = lanes // bins
    groups = held // per_row
    per_owner = slices * views * groups
    wide[...] = wire[...].astype(F32)
    mask = (
        lax.broadcasted_iota(jnp.int32, (per_row, lanes), 1) // bins
        == lax.broadcasted_iota(jnp.int32, (per_row, lanes), 0)
    )
    block = min(BLOCK, cells)
    edges = range(block, cells, block)
    narrow_edges = range(NARROW, cells, NARROW)
    ends_x = [[corner_rows(edge_x[v, n], cells) for n in range(len(narrow_edges))] for v in range(views)]
    stores = []

    def line(z, v, first):
        row = first // held * per_owner + (z * views + v) * groups + first % held // per_row
        return jnp.where(mask, jnp.broadcast_to(wide[pl.ds(row, 1), :], (per_row, lanes)), 0.0)

    def spread_frames(z):
        for v in range(views):
            back = jnp.concatenate([line(z, v, n) for n in range(0, cells, per_row)], axis=0)
            frames[z * views + v] = dot(toft[v], back.astype(BF16), NT).astype(BF16)

    def edge_frames(n, edge):
        extra = []
        for v in range(views):
            near = [line(z, v, first) for z in range(slices) for first in (edge - 8, edge)]
            weights = jnp.concatenate([tof[v]] * per_row, axis=0)
            near = dot(jnp.concatenate(near, axis=0).astype(BF16), weights).astype(BF16).astype(F32)
            above, below = corner_columns(edge_y[v, n], cells)
            for z in range(slices):
                own = near[16 * z : 16 * z + 16]
                extra.append(sum(above[m] * own[8 + m : 9 + m] for m in range(BAND)))
                extra.append(sum(below[m] * own[7 - m : 8 - m] for m in range(BAND)))
        turned[n] = jnp.concatenate(extra, axis=0).T

    def unrotate(z):
        for v in range(views):
            i = z * views + v
            parts = [
                dot(frames[i, :, at : at + block], ryt[v, at : at + block, at : at + block])
                for at in range(0, cells, block)
            ]
            for n in range(len(edges)):
                extra = turned[n]
                lane = lax.broadcasted_iota(jnp.int32, extra.shape, 1)
                extra = pltpu.roll(extra, (120 - 16 * (v * slices + z)) % 128, 1)
                left, right = parts[n], parts[n + 1]
                parts[n] = jnp.concatenate(
                    [left[:, :-128], left[:, -128:] + jnp.where(lane >= 120, extra, 0.0)], axis=1
                )
                parts[n + 1] = jnp.concatenate(
                    [right[:, :128] + jnp.where(lane < 8, extra, 0.0), right[:, 128:]], axis=1
                )
            for n, part in enumerate(parts):
                part = part.astype(BF16)
                for w in range(cells // NARROW):
                    unrotated[z, w, v * NARROW : (v + 1) * NARROW, n * block : (n + 1) * block] = part[
                        w * NARROW : (w + 1) * NARROW
                    ]

    def finish_slice(z):
        for w in range(cells // NARROW):
            part = dot(strips_x[w], unrotated[z, w])
            first, last = part[:8], part[-8:]
            for v in range(views):
                if w > 0:
                    end = (v + 1) * NARROW
                    near = unrotated[z, w - 1, end - 16 : end, :].astype(F32)
                    for m in range(BAND):
                        first += ends_x[v][w - 1][1][m] * near[15 - m : 16 - m]
                if (w + 1) * NARROW < cells:
                    near = unrotated[z, w + 1, v * NARROW : v * NARROW + 16, :].astype(F32)
                    for m in range(BAND):
                        last += ends_x[v][w][0][m] * near[m : m + 1]
            part = jnp.concatenate([first, part[8:-8], last], axis=0)
            rows = slice(w * NARROW, (w + 1) * NARROW)
            if finish:
                part = image[z, rows, :] * part / sensitivity[z, rows, :]
            result[z, rows, :] = part
            if z == slices - 1:
                keep(result.at[z, rows], out_hbm.at[z, rows])
        if z < slices - 1:
            keep(result.at[z], out_hbm.at[z])

    def keep(source, target):
        store = pltpu.make_async_copy(source, target, sems.at[len(stores)])
        store.start()
        stores.append(store)

    spread_frames(0)
    for n, edge in enumerate(edges):
        edge_frames(n, edge)
    for z in range(slices):
        unrotate(z)
        if z + 1 < slices:
            spread_frames(z + 1)
        finish_slice(z)
    for store in stores:
        store.wait()


def local(view_size, image, sensitivity, resample_x, resample_y, tof_kernel, axial_mix, background, counts):
    views, bins, cells = tof_kernel.shape
    slices, nx, ny = image.shape
    held, planes = background.shape[2:]
    owners = planes // slices
    lanes = slices * views * bins
    vmem = pl.BlockSpec(memory_space=pltpu.VMEM)
    anywhere = pl.BlockSpec(memory_space=pl.ANY)

    block = min(BLOCK, nx)
    narrow = nx // NARROW
    wire, current, strips_x, ryt, edge_y, edge_x, toft, tof = pl.pallas_call(
        functools.partial(forward_kernel, views, slices, bins),
        in_specs=[anywhere] * 4,
        out_specs=[vmem] * 8,
        out_shape=[
            pltpu.VMEM((ny, lanes), BF16),
            pltpu.VMEM(image.shape, F32),
            pltpu.VMEM((narrow, NARROW, views * NARROW), BF16),
            pltpu.VMEM(resample_y.shape, BF16),
            pltpu.VMEM((views, max(ny // block - 1, 1), 2 * NEAR, 256), BF16),
            pltpu.VMEM((views, max(narrow - 1, 1), 2 * NEAR, 256), BF16),
            pltpu.VMEM((views, nx, lanes), BF16),
            pltpu.VMEM(tof_kernel.shape, BF16),
        ],
        scratch_shapes=[
            pltpu.VMEM(resample_x.shape, BF16),
            pltpu.VMEM(resample_y.shape, BF16),
            pltpu.SemaphoreType.DMA((4 * (nx // block) - 1 + slices,)),
        ],
        compiler_params=pltpu.CompilerParams(vmem_limit_bytes=VMEM_LIMIT),
        name="project",
    )(*map(in_hbm, (image, resample_x, resample_y, tof_kernel)))
    wire = lax.all_to_all(
        wire.reshape(owners, held, lanes), "slab", 0, 0, tiled=True
    ).reshape(ny, lanes)

    per_owner = slices * views * (held * bins // lanes)
    back = pl.pallas_call(
        functools.partial(middle_kernel, views, slices, bins, owners, held),
        out_specs=vmem,
        out_shape=pltpu.VMEM((owners * per_owner, lanes), BF16),
        scratch_shapes=[
            pltpu.VMEM((planes, planes), F32),
            pltpu.VMEM((owners * per_owner, lanes), F32),
            pltpu.VMEM((owners * held, lanes), F32),
        ],
        compiler_params=pltpu.CompilerParams(vmem_limit_bytes=VMEM_LIMIT),
        cost_estimate=pl.CostEstimate(flops=0, bytes_accessed=40 * 1024 * 1024, transcendentals=0),
        name="compare",
    )(
        wire,
        axial_mix,
        background.reshape(-1, planes),
        counts.reshape(-1, planes),
    )
    back = lax.all_to_all(
        back.reshape(owners, per_owner, lanes), "slab", 0, 0, tiled=True
    ).reshape(owners * per_owner, lanes)

    finish = view_size == 1
    operands = [back, tof, toft, ryt, strips_x, edge_y, edge_x]
    if finish:
        operands += [current, sensitivity]
    result = pl.pallas_call(
        functools.partial(backward_kernel, views, slices, bins, owners, held, finish),
        in_specs=[vmem] * len(operands),
        out_specs=anywhere,
        out_shape=jax.ShapeDtypeStruct((slices, nx, ny), F32),
        scratch_shapes=[
            pltpu.VMEM(image.shape, F32),
            pltpu.VMEM((owners * per_owner, lanes), F32),
            pltpu.VMEM((slices * views, nx, ny), BF16),
            pltpu.VMEM((slices, narrow, views * NARROW, ny), BF16),
            pltpu.VMEM((max(ny // block - 1, 1), nx, 16 * slices * views), F32),
            pltpu.SemaphoreType.DMA((slices - 1 + narrow,)),
        ],
        compiler_params=pltpu.CompilerParams(vmem_limit_bytes=VMEM_LIMIT),
        name="backproject",
    )(*operands)
    if finish:
        return result
    gradient = lax.psum_scatter(result, "view", scatter_dimension=1, tiled=True)
    own_rows = nx // view_size
    own = lax.dynamic_slice_in_dim(image, lax.axis_index("view") * own_rows, own_rows, 1)
    return own * gradient / sensitivity


def solution(mesh):
    in_specs = (
        P("slab", None, None),
        P("slab", "view", None),
        P("view", None, None),
        P("view", None, None),
        P("view", None, None),
        P("view", None, None),
        P("view", None, "slab", None),
        P("view", None, "slab", None),
    )
    out_specs = P("slab", "view", None)
    return jax.shard_map(
        functools.partial(local, mesh.shape["view"]),
        mesh=mesh,
        in_specs=in_specs,
        out_specs=out_specs,
        check_vma=False,
    )
```

```python
import functools

import jax
import jax.numpy as jnp
from jax import lax
from jax.experimental import pallas as pl
from jax.experimental.pallas import tpu as pltpu
from jax.sharding import PartitionSpec as P

F32, BF16 = jnp.float32, jnp.bfloat16
VMEM_LIMIT = 24 * 1024 * 1024
FIRST_LIMIT = 60 * 1024 * 1024
BLOCK, NARROW, BAND, NEAR = 256, 128, 3, 16
POWER, OFFSET = 41.5, 86.3
NN = (((1,), (0,)), ((), ()))
NT = (((1,), (1,)), ((), ()))


def dot(a, b, dims=NN):
    return lax.dot_general(a, b, dims, preferred_element_type=F32)


def halves(x):
    high = x.astype(BF16)
    return high, (x - high.astype(F32)).astype(BF16)


def dot3(a, b, dims=NN):
    ah, al = halves(a)
    bh, bl = halves(b)
    return dot(ah, bh, dims) + (dot(ah, bl, dims) + dot(al, bh, dims))


def encode(x):
    place = POWER * jnp.log(1.0 + 2.0 * x) - 2.0 * OFFSET
    size = jnp.exp(jnp.abs(place) - OFFSET)
    return jnp.where(place < 0.0, -size, size).astype(BF16)


def decode(y):
    y = y.astype(F32)
    size = jnp.log(jnp.abs(y)) + OFFSET
    place = jnp.where(y < 0.0, -size, size)
    return 0.5 * jnp.exp((place + 2.0 * OFFSET) * (1.0 / POWER)) - 0.5


def in_hbm(x):
    return pltpu.with_memory_space_constraint(x, pltpu.HBM)


def forward_kernel(
    views, slices, bins, image_hbm, rx_hbm, ry_hbm, tof_hbm,
    out, image, strips_x, ryt, edge_y, edge_x, toft, tof, rx, ry, along, rotated, sems,
):
    cells = rx.shape[1]
    block = min(BLOCK, cells)

    def band(source, target, edge, step):
        copies = []
        for at in range(0, cells, block):
            place = (slice(None), pl.ds(at, block), pl.ds(at, block))
            copies.append((source.at[place], target.at[place]))
            if at > 0:
                window = (slice(None), pl.ds(at - NEAR, 2 * NEAR), pl.ds(at - 128, 256))
                copies.append((source.at[window], edge.at[:, at // step - 1]))
        return copies

    images = [(image_hbm.at[z], image.at[z]) for z in range(slices)]
    groups = [band(ry_hbm, ry, edge_y, block), images[:1]]
    groups += [[(tof_hbm, tof)] + band(rx_hbm, rx, edge_x, NARROW)]
    groups += [[pair] for pair in images[1:]]
    loads, n = [], 0
    for group in groups:
        loads.append([pltpu.make_async_copy(*pair, sems.at[n + i]) for i, pair in enumerate(group)])
        n += len(group)
    for load in sum(loads, []):
        load.start()
    loads = iter(loads)

    def arrive():
        for load in next(loads):
            load.wait()

    per_row = toft.shape[2] // bins
    edges = range(block, cells, block)
    integrals = []

    def along_second(z):
        low = image[z].astype(BF16)
        extra = [dot(low[:, e - 128 : e + 128], corners[n]) for n, e in enumerate(edges)]
        for v in range(views):
            parts = [
                dot(low[:, at : at + block], ry[v, at : at + block, at : at + block])
                for at in range(0, cells, block)
            ]
            parts = add_sides(parts, extra, 16 * v)
            for n, part in enumerate(parts):
                along[z * views + v, :, n * block : (n + 1) * block] = part.astype(BF16)

    def along_first(z):
        for v in range(views):
            i = z * views + v
            parts = [
                dot(rx[v, at : at + block, at : at + block], along[i, at : at + block, :])
                for at in range(0, cells, block)
            ]
            for n, e in enumerate(edges):
                above, below = sides[v][n]
                near = along[i, e - 16 : e + 16, :].astype(F32)
                last, first = parts[n][-8:], parts[n + 1][:8]
                for m in range(BAND):
                    last += above[m] * near[16 + m : 17 + m]
                    first += below[m] * near[15 - m : 16 - m]
                parts[n] = jnp.concatenate([parts[n][:-8], last], axis=0)
                parts[n + 1] = jnp.concatenate([first, parts[n + 1][8:]], axis=0)
            for n, part in enumerate(parts):
                rotated[i, n * block : (n + 1) * block, :] = part.astype(BF16)

    def along_rays(z):
        for v in range(views):
            integrals.append(dot(tof[v], rotated[z * views + v]))

    arrive()
    corners = []
    for n in range(len(edges)):
        near = [corner(edge_y[v, n])[:, 120:136] for v in range(views)]
        near = jnp.concatenate(near + [jnp.zeros((2 * NEAR, 128 - 16 * views), F32)], axis=1)
        above = jnp.zeros((128 - NEAR, 128), F32)
        corners.append(jnp.concatenate([above, near, above], axis=0).astype(BF16))
    arrive()
    along_second(0)
    arrive()
    between = block // NARROW
    sides = [
        [corner_columns(edge_x[v, (n + 1) * between - 1], cells) for n in range(len(edges))]
        for v in range(views)
    ]
    along_first(0)
    for z in range(1, slices):
        arrive()
        along_second(z)
        along_rays(z - 1)
        along_first(z)
        if z == 1:
            for v in range(views):
                for n, at in enumerate(range(0, cells, NARROW)):
                    strips_x[n, :, v * NARROW : (v + 1) * NARROW] = rx[
                        v, at : at + NARROW, at : at + NARROW
                    ].T
                    if at % block > 0:
                        edge_x[v, n - 1] = rx[v, at - NEAR : at + NEAR, at - 128 : at + 128]
        if z == min(2, slices - 1):
            for v in range(views):
                toft[v] = jnp.concatenate([tof[v]] * per_row, axis=0).T
                for at in range(0, cells, block):
                    here = slice(at, at + block)
                    ryt[v, here, here] = ry[v, here, here].T
    along_rays(slices - 1)
    out[...] = encode(jnp.concatenate(integrals, axis=0).T)


def add_sides(parts, extra, spot):
    parts = list(parts)
    for n, columns in enumerate(extra):
        lane = lax.broadcasted_iota(jnp.int32, columns.shape, 1)
        columns = pltpu.roll(columns, (120 - spot) % 128, 1)
        left, right = parts[n], parts[n + 1]
        parts[n] = jnp.concatenate(
            [left[:, :-128], left[:, -128:] + jnp.where(lane >= 120, columns, 0.0)], axis=1
        )
        parts[n + 1] = jnp.concatenate(
            [right[:, :128] + jnp.where(lane < 8, columns, 0.0), right[:, 128:]], axis=1
        )
    return parts


def swap_blocks(parts, width):
    n = len(parts)
    lane = lax.broadcasted_iota(jnp.int32, parts[0].shape, 1) // width
    step = 1
    while step < n:
        low = (lane // step) % 2 == 0
        new = list(parts)
        for i in range(n):
            if (i // step) % 2 == 0:
                a, b = parts[i], parts[i + step]
                shift = step * width
                new[i] = jnp.where(low, a, pltpu.roll(b, shift, 1))
                new[i + step] = jnp.where(
                    low, pltpu.roll(a, a.shape[1] - shift, 1), b
                )
        parts = new
        step *= 2
    return parts


def middle_kernel(views, slices, bins, owners, held, wire, mix, background, counts, out, turned, spread, sums_in):
    rows = views * bins
    lanes = slices * rows
    sums_in[...] = decode(wire[...])
    blocks = []
    for first in range(0, held, slices):
        parts = [
            sums_in[pl.ds(first + i, owners, stride=held), :] for i in range(slices)
        ]
        blocks.append(jnp.concatenate(swap_blocks(parts, rows), axis=0).T)
    for v in range(views):
        turned[...] = mix[v].T
        mixed = jnp.concatenate(
            [turned[pl.ds(s, owners, stride=slices), :] for s in range(slices)], axis=0
        )
        sums = jnp.concatenate(
            [
                blocks[j // slices][
                    (j % slices) * rows + v * bins : (j % slices) * rows + (v + 1) * bins
                ]
                for j in range(held)
            ],
            axis=0,
        )
        base = v * bins * held
        added = jnp.concatenate(
            [background[pl.ds(base + j, bins, stride=held), :] for j in range(held)], axis=0
        )
        seen = jnp.concatenate(
            [counts[pl.ds(base + j, bins, stride=held), :] for j in range(held)], axis=0
        )
        ratios = seen.astype(F32) / (added + dot3(sums, mixed))
        back = dot3(mixed, ratios, NT)
        groups = held * bins // lanes
        for s in range(slices):
            for g in range(groups):
                spread[pl.ds((s * views + v) * groups + g, owners, stride=slices * views * groups), :] = back[
                    s * owners : (s + 1) * owners, g * lanes : (g + 1) * lanes
                ]
    out[...] = spread[...].astype(BF16)


def corner(window):
    window = window.astype(F32)
    row = lax.broadcasted_iota(jnp.int32, window.shape, 0) < window.shape[0] // 2
    column = lax.broadcasted_iota(jnp.int32, window.shape, 1) < window.shape[1] // 2
    return jnp.where(row != column, window, 0.0)


def corner_columns(window, width):
    near = corner(window)[NEAR - 8 : NEAR + 8]
    spread = lambda rows, n: jnp.broadcast_to(near[rows, n : n + 1], (8, width))
    return (
        [spread(slice(0, 8), 128 + n) for n in range(BAND)],
        [spread(slice(8, 16), 127 - n) for n in range(BAND)],
    )


def corner_rows(window, width):
    near = corner(window)[:, 120:136]
    flat = jnp.concatenate([near, jnp.zeros((2 * NEAR, 112), F32)], axis=1)
    turned = jnp.concatenate([flat, jnp.zeros((128 - 2 * NEAR, 128), F32)], axis=0).T
    spread = lambda rows, n: jnp.broadcast_to(turned[rows, n : n + 1], (8, width))
    return (
        [spread(slice(0, 8), NEAR + n) for n in range(BAND)],
        [spread(slice(8, 16), NEAR - 1 - n) for n in range(BAND)],
    )


def backward_kernel(views, slices, bins, owners, held, finish, *refs):
    wire, tof, toft, ryt, strips_x, edge_y, edge_x = refs[:7]
    if finish:
        image, sensitivity = refs[7:9]
    out_hbm, result, wide, frames, unrotated, turned, sems = refs[-7:]

    cells = ryt.shape[1]
    lanes = wire.shape[1]
    per_row = lanes // bins
    groups = held // per_row
    per_owner = slices * views * groups
    wide[...] = wire[...].astype(F32)
    mask = (
        lax.broadcasted_iota(jnp.int32, (per_row, lanes), 1) // bins
        == lax.broadcasted_iota(jnp.int32, (per_row, lanes), 0)
    )
    block = min(BLOCK, cells)
    edges = range(block, cells, block)
    narrow_edges = range(NARROW, cells, NARROW)
    ends_x = [[corner_rows(edge_x[v, n], cells) for n in range(len(narrow_edges))] for v in range(views)]
    stores = []

    def line(z, v, first):
        row = first // held * per_owner + (z * views + v) * groups + first % held // per_row
        return jnp.where(mask, jnp.broadcast_to(wide[pl.ds(row, 1), :], (per_row, lanes)), 0.0)

    def spread_frames(z):
        for v in range(views):
            back = jnp.concatenate([line(z, v, n) for n in range(0, cells, per_row)], axis=0)
            frames[z * views + v] = dot(toft[v], back.astype(BF16), NT).astype(BF16)

    def edge_frames(n, edge):
        extra = []
        for v in range(views):
            near = [line(z, v, first) for z in range(slices) for first in (edge - 8, edge)]
            weights = jnp.concatenate([tof[v]] * per_row, axis=0)
            near = dot(jnp.concatenate(near, axis=0).astype(BF16), weights).astype(BF16).astype(F32)
            above, below = corner_columns(edge_y[v, n], cells)
            for z in range(slices):
                own = near[16 * z : 16 * z + 16]
                extra.append(sum(above[m] * own[8 + m : 9 + m] for m in range(BAND)))
                extra.append(sum(below[m] * own[7 - m : 8 - m] for m in range(BAND)))
        turned[n] = jnp.concatenate(extra, axis=0).T

    def unrotate(z):
        for v in range(views):
            i = z * views + v
            parts = [
                dot(frames[i, :, at : at + block], ryt[v, at : at + block, at : at + block])
                for at in range(0, cells, block)
            ]
            parts = add_sides(parts, [turned[n] for n in range(len(edges))], 16 * (v * slices + z))
            for n, part in enumerate(parts):
                part = part.astype(BF16)
                for w in range(cells // NARROW):
                    unrotated[z, w, v * NARROW : (v + 1) * NARROW, n * block : (n + 1) * block] = part[
                        w * NARROW : (w + 1) * NARROW
                    ]

    def finish_slice(z):
        for w in range(cells // NARROW):
            part = dot(strips_x[w], unrotated[z, w])
            first, last = part[:8], part[-8:]
            for v in range(views):
                if w > 0:
                    end = (v + 1) * NARROW
                    near = unrotated[z, w - 1, end - 16 : end, :].astype(F32)
                    for m in range(BAND):
                        first += ends_x[v][w - 1][1][m] * near[15 - m : 16 - m]
                if (w + 1) * NARROW < cells:
                    near = unrotated[z, w + 1, v * NARROW : v * NARROW + 16, :].astype(F32)
                    for m in range(BAND):
                        last += ends_x[v][w][0][m] * near[m : m + 1]
            part = jnp.concatenate([first, part[8:-8], last], axis=0)
            rows = slice(w * NARROW, (w + 1) * NARROW)
            if finish:
                part = image[z, rows, :] * part / sensitivity[z, rows, :]
            result[z, rows, :] = part
            if z == slices - 1:
                keep(result.at[z, rows], out_hbm.at[z, rows])
        if z < slices - 1:
            keep(result.at[z], out_hbm.at[z])

    def keep(source, target):
        store = pltpu.make_async_copy(source, target, sems.at[len(stores)])
        store.start()
        stores.append(store)

    spread_frames(0)
    for n, edge in enumerate(edges):
        edge_frames(n, edge)
    for z in range(slices):
        unrotate(z)
        if z + 1 < slices:
            spread_frames(z + 1)
        finish_slice(z)
    for store in stores:
        store.wait()


def local(view_size, image, sensitivity, resample_x, resample_y, tof_kernel, axial_mix, background, counts):
    views, bins, cells = tof_kernel.shape
    slices, nx, ny = image.shape
    held, planes = background.shape[2:]
    owners = planes // slices
    lanes = slices * views * bins
    vmem = pl.BlockSpec(memory_space=pltpu.VMEM)
    anywhere = pl.BlockSpec(memory_space=pl.ANY)

    block = min(BLOCK, nx)
    narrow = nx // NARROW
    wire, current, strips_x, ryt, edge_y, edge_x, toft, tof = pl.pallas_call(
        functools.partial(forward_kernel, views, slices, bins),
        in_specs=[anywhere] * 4,
        out_specs=[vmem] * 8,
        out_shape=[
            pltpu.VMEM((ny, lanes), BF16),
            pltpu.VMEM(image.shape, F32),
            pltpu.VMEM((narrow, NARROW, views * NARROW), BF16),
            pltpu.VMEM(resample_y.shape, BF16),
            pltpu.VMEM((views, max(ny // block - 1, 1), 2 * NEAR, 256), BF16),
            pltpu.VMEM((views, max(narrow - 1, 1), 2 * NEAR, 256), BF16),
            pltpu.VMEM((views, nx, lanes), BF16),
            pltpu.VMEM(tof_kernel.shape, BF16),
        ],
        scratch_shapes=[
            pltpu.VMEM(resample_x.shape, BF16),
            pltpu.VMEM(resample_y.shape, BF16),
            pltpu.VMEM((slices * views, nx, ny), BF16),
            pltpu.VMEM((slices * views, nx, ny), BF16),
            pltpu.SemaphoreType.DMA((4 * (nx // block) - 1 + slices,)),
        ],
        compiler_params=pltpu.CompilerParams(vmem_limit_bytes=VMEM_LIMIT),
        name="project",
    )(*map(in_hbm, (image, resample_x, resample_y, tof_kernel)))
    wire = lax.all_to_all(
        wire.reshape(owners, held, lanes), "slab", 0, 0, tiled=True
    ).reshape(ny, lanes)

    per_owner = slices * views * (held * bins // lanes)
    back = pl.pallas_call(
        functools.partial(middle_kernel, views, slices, bins, owners, held),
        out_specs=vmem,
        out_shape=pltpu.VMEM((owners * per_owner, lanes), BF16),
        scratch_shapes=[
            pltpu.VMEM((planes, planes), F32),
            pltpu.VMEM((owners * per_owner, lanes), F32),
            pltpu.VMEM((owners * held, lanes), F32),
        ],
        compiler_params=pltpu.CompilerParams(vmem_limit_bytes=VMEM_LIMIT),
        cost_estimate=pl.CostEstimate(flops=0, bytes_accessed=40 * 1024 * 1024, transcendentals=0),
        name="compare",
    )(
        wire,
        axial_mix,
        background.reshape(-1, planes),
        counts.reshape(-1, planes),
    )
    back = lax.all_to_all(
        back.reshape(owners, per_owner, lanes), "slab", 0, 0, tiled=True
    ).reshape(owners * per_owner, lanes)

    finish = view_size == 1
    operands = [back, tof, toft, ryt, strips_x, edge_y, edge_x]
    if finish:
        operands += [current, sensitivity]
    result = pl.pallas_call(
        functools.partial(backward_kernel, views, slices, bins, owners, held, finish),
        in_specs=[vmem] * len(operands),
        out_specs=anywhere,
        out_shape=jax.ShapeDtypeStruct((slices, nx, ny), F32),
        scratch_shapes=[
            pltpu.VMEM(image.shape, F32),
            pltpu.VMEM((owners * per_owner, lanes), F32),
            pltpu.VMEM((slices * views, nx, ny), BF16),
            pltpu.VMEM((slices, narrow, views * NARROW, ny), BF16),
            pltpu.VMEM((max(ny // block - 1, 1), nx, 16 * slices * views), F32),
            pltpu.SemaphoreType.DMA((slices - 1 + narrow,)),
        ],
        compiler_params=pltpu.CompilerParams(vmem_limit_bytes=VMEM_LIMIT),
        name="backproject",
    )(*operands)
    if finish:
        return result
    gradient = lax.psum_scatter(result, "view", scatter_dimension=1, tiled=True)
    own_rows = nx // view_size
    own = lax.dynamic_slice_in_dim(image, lax.axis_index("view") * own_rows, own_rows, 1)
    return own * gradient / sensitivity


def solution(mesh):
    in_specs = (
        P("slab", None, None),
        P("slab", "view", None),
        P("view", None, None),
        P("view", None, None),
        P("view", None, None),
        P("view", None, None),
        P("view", None, "slab", None),
        P("view", None, "slab", None),
    )
    out_specs = P("slab", "view", None)
    return jax.shard_map(
        functools.partial(local, mesh.shape["view"]),
        mesh=mesh,
        in_specs=in_specs,
        out_specs=out_specs,
        check_vma=False,
    )
```

```python
import functools

import jax
import jax.numpy as jnp
from jax import lax
from jax.experimental import pallas as pl
from jax.experimental.pallas import tpu as pltpu
from jax.sharding import PartitionSpec as P

F32, BF16 = jnp.float32, jnp.bfloat16
VMEM_LIMIT = 24 * 1024 * 1024
FIRST_LIMIT = 60 * 1024 * 1024
BLOCK, NARROW, BAND, NEAR = 256, 128, 3, 16
POWER, OFFSET = 41.5, 86.3
NN = (((1,), (0,)), ((), ()))
NT = (((1,), (1,)), ((), ()))


def dot(a, b, dims=NN):
    return lax.dot_general(a, b, dims, preferred_element_type=F32)


def halves(x):
    high = x.astype(BF16)
    return high, (x - high.astype(F32)).astype(BF16)


def dot3(a, b, dims=NN):
    ah, al = halves(a)
    bh, bl = halves(b)
    return dot(ah, bh, dims) + (dot(ah, bl, dims) + dot(al, bh, dims))


def encode(x):
    place = POWER * jnp.log(1.0 + 2.0 * x) - 2.0 * OFFSET
    size = jnp.exp(jnp.abs(place) - OFFSET)
    return jnp.where(place < 0.0, -size, size)


def decode(y):
    y = y.astype(F32)
    size = jnp.log(jnp.abs(y)) + OFFSET
    place = jnp.where(y < 0.0, -size, size)
    return 0.5 * jnp.exp((place + 2.0 * OFFSET) * (1.0 / POWER)) - 0.5


def in_hbm(x):
    return pltpu.with_memory_space_constraint(x, pltpu.HBM)


def forward_kernel(
    views, slices, bins, image_hbm, rx_hbm, ry_hbm, tof_hbm,
    out, image, strips_x, ryt, edge_y, edge_x, toft, tof, rx, ry, along, rotated, sems,
):
    cells = rx.shape[1]
    block = min(BLOCK, cells)

    def band(source, target, edge, step):
        copies = []
        for at in range(0, cells, block):
            place = (slice(None), pl.ds(at, block), pl.ds(at, block))
            copies.append((source.at[place], target.at[place]))
            if at > 0:
                window = (slice(None), pl.ds(at - NEAR, 2 * NEAR), pl.ds(at - 128, 256))
                copies.append((source.at[window], edge.at[:, at // step - 1]))
        return copies

    images = [(image_hbm.at[z], image.at[z]) for z in range(slices)]
    top, bottom = pl.ds(0, block), pl.ds(block, cells - block)
    groups = [band(ry_hbm, ry, edge_y, block) + [(image_hbm.at[0, top], image.at[0, top])]]
    groups += [[(image_hbm.at[0, bottom], image.at[0, bottom])]]
    groups += [[(tof_hbm, tof)] + band(rx_hbm, rx, edge_x, NARROW)]
    groups += [[pair] for pair in images[1:]]
    loads, n = [], 0
    for group in groups:
        loads.append([pltpu.make_async_copy(*pair, sems.at[n + i]) for i, pair in enumerate(group)])
        n += len(group)
    for load in sum(loads, []):
        load.start()
    loads = iter(loads)

    def arrive():
        for load in next(loads):
            load.wait()

    per_row = toft.shape[2] // bins
    edges = range(block, cells, block)
    coded = []

    def along_second(z, rows=slice(None)):
        low = image[z, rows].astype(BF16)
        extra = [dot(low[:, e - 128 : e + 128], corners[n]) for n, e in enumerate(edges)]
        for v in range(views):
            parts = [
                dot(low[:, at : at + block], ry[v, at : at + block, at : at + block])
                for at in range(0, cells, block)
            ]
            parts = add_sides(parts, extra, 16 * v)
            for n, part in enumerate(parts):
                along[z * views + v, rows, n * block : (n + 1) * block] = part.astype(BF16)

    def along_first(z):
        for v in range(views):
            i = z * views + v
            parts = [
                dot(rx[v, at : at + block, at : at + block], along[i, at : at + block, :])
                for at in range(0, cells, block)
            ]
            for n, e in enumerate(edges):
                above, below = sides[v][n]
                near = along[i, e - 16 : e + 16, :].astype(F32)
                last, first = parts[n][-8:], parts[n + 1][:8]
                for m in range(BAND):
                    last += above[m] * near[16 + m : 17 + m]
                    first += below[m] * near[15 - m : 16 - m]
                parts[n] = jnp.concatenate([parts[n][:-8], last], axis=0)
                parts[n + 1] = jnp.concatenate([first, parts[n + 1][8:]], axis=0)
            for n, part in enumerate(parts):
                rotated[i, n * block : (n + 1) * block, :] = part.astype(BF16)

    def along_rays(z):
        for v in range(views):
            coded.append(encode(dot(tof[v], rotated[z * views + v])))

    arrive()
    corners = []
    for n in range(len(edges)):
        near = [corner(edge_y[v, n])[:, 120:136] for v in range(views)]
        near = jnp.concatenate(near + [jnp.zeros((2 * NEAR, 128 - 16 * views), F32)], axis=1)
        above = jnp.zeros((128 - NEAR, 128), F32)
        corners.append(jnp.concatenate([above, near, above], axis=0).astype(BF16))
    along_second(0, slice(0, block))
    arrive()
    along_second(0, slice(block, cells))
    arrive()
    between = block // NARROW
    sides = [
        [corner_columns(edge_x[v, (n + 1) * between - 1], cells) for n in range(len(edges))]
        for v in range(views)
    ]
    for z in range(1, slices):
        arrive()
        along_second(z)
        along_first(z - 1)
        if z > 1:
            along_rays(z - 2)
        if z == 1:
            for v in range(views):
                for n, at in enumerate(range(0, cells, NARROW)):
                    strips_x[n, :, v * NARROW : (v + 1) * NARROW] = rx[
                        v, at : at + NARROW, at : at + NARROW
                    ].T
                    if at % block > 0:
                        edge_x[v, n - 1] = rx[v, at - NEAR : at + NEAR, at - 128 : at + 128]
        if z == min(2, slices - 1):
            for v in range(views):
                toft[v] = jnp.concatenate([tof[v]] * per_row, axis=0).T
                for at in range(0, cells, block):
                    here = slice(at, at + block)
                    ryt[v, here, here] = ry[v, here, here].T
    along_rays(slices - 2)
    along_first(slices - 1)
    along_rays(slices - 1)
    out[...] = jnp.concatenate(coded, axis=0).T.astype(BF16)


def add_sides(parts, extra, spot):
    parts = list(parts)
    for n, columns in enumerate(extra):
        lane = lax.broadcasted_iota(jnp.int32, columns.shape, 1)
        columns = pltpu.roll(columns, (120 - spot) % 128, 1)
        left, right = parts[n], parts[n + 1]
        parts[n] = jnp.concatenate(
            [left[:, :-128], left[:, -128:] + jnp.where(lane >= 120, columns, 0.0)], axis=1
        )
        parts[n + 1] = jnp.concatenate(
            [right[:, :128] + jnp.where(lane < 8, columns, 0.0), right[:, 128:]], axis=1
        )
    return parts


def swap_blocks(parts, width):
    n = len(parts)
    lane = lax.broadcasted_iota(jnp.int32, parts[0].shape, 1) // width
    step = 1
    while step < n:
        low = (lane // step) % 2 == 0
        new = list(parts)
        for i in range(n):
            if (i // step) % 2 == 0:
                a, b = parts[i], parts[i + step]
                shift = step * width
                new[i] = jnp.where(low, a, pltpu.roll(b, shift, 1))
                new[i + step] = jnp.where(
                    low, pltpu.roll(a, a.shape[1] - shift, 1), b
                )
        parts = new
        step *= 2
    return parts


def middle_kernel(views, slices, bins, owners, held, wire, mix, background, counts, out, turned, spread, sums_in):
    rows = views * bins
    lanes = slices * rows
    sums_in[...] = decode(wire[...])
    blocks = []
    for first in range(0, held, slices):
        parts = [
            sums_in[pl.ds(first + i, owners, stride=held), :] for i in range(slices)
        ]
        blocks.append(jnp.concatenate(swap_blocks(parts, rows), axis=0).T)
    for v in range(views):
        turned[...] = mix[v].T
        mixed = jnp.concatenate(
            [turned[pl.ds(s, owners, stride=slices), :] for s in range(slices)], axis=0
        )
        sums = jnp.concatenate(
            [
                blocks[j // slices][
                    (j % slices) * rows + v * bins : (j % slices) * rows + (v + 1) * bins
                ]
                for j in range(held)
            ],
            axis=0,
        )
        base = v * bins * held
        added = jnp.concatenate(
            [background[pl.ds(base + j, bins, stride=held), :] for j in range(held)], axis=0
        )
        seen = jnp.concatenate(
            [counts[pl.ds(base + j, bins, stride=held), :] for j in range(held)], axis=0
        )
        ratios = seen.astype(F32) / (added + dot3(sums, mixed))
        back = dot3(mixed, ratios, NT)
        groups = held * bins // lanes
        for s in range(slices):
            for g in range(groups):
                spread[pl.ds((s * views + v) * groups + g, owners, stride=slices * views * groups), :] = back[
                    s * owners : (s + 1) * owners, g * lanes : (g + 1) * lanes
                ]
    out[...] = spread[...].astype(BF16)


def corner(window):
    window = window.astype(F32)
    row = lax.broadcasted_iota(jnp.int32, window.shape, 0) < window.shape[0] // 2
    column = lax.broadcasted_iota(jnp.int32, window.shape, 1) < window.shape[1] // 2
    return jnp.where(row != column, window, 0.0)


def corner_columns(window, width):
    near = corner(window)[NEAR - 8 : NEAR + 8]
    spread = lambda rows, n: jnp.broadcast_to(near[rows, n : n + 1], (8, width))
    return (
        [spread(slice(0, 8), 128 + n) for n in range(BAND)],
        [spread(slice(8, 16), 127 - n) for n in range(BAND)],
    )


def corner_rows(window, width):
    near = corner(window)[:, 120:136]
    flat = jnp.concatenate([near, jnp.zeros((2 * NEAR, 112), F32)], axis=1)
    turned = jnp.concatenate([flat, jnp.zeros((128 - 2 * NEAR, 128), F32)], axis=0).T
    spread = lambda rows, n: jnp.broadcast_to(turned[rows, n : n + 1], (8, width))
    return (
        [spread(slice(0, 8), NEAR + n) for n in range(BAND)],
        [spread(slice(8, 16), NEAR - 1 - n) for n in range(BAND)],
    )


def backward_kernel(views, slices, bins, owners, held, finish, *refs):
    wire, tof, toft, ryt, strips_x, edge_y, edge_x = refs[:7]
    if finish:
        image, sensitivity = refs[7:9]
    out_hbm, result, wide, frames, unrotated, turned, sems = refs[-7:]

    cells = ryt.shape[1]
    lanes = wire.shape[1]
    per_row = lanes // bins
    groups = held // per_row
    per_owner = slices * views * groups
    wide[...] = wire[...].astype(F32)
    mask = (
        lax.broadcasted_iota(jnp.int32, (per_row, lanes), 1) // bins
        == lax.broadcasted_iota(jnp.int32, (per_row, lanes), 0)
    )
    block = min(BLOCK, cells)
    edges = range(block, cells, block)
    narrow_edges = range(NARROW, cells, NARROW)
    ends_x = [[corner_rows(edge_x[v, n], cells) for n in range(len(narrow_edges))] for v in range(views)]
    stores = []

    def line(z, v, first):
        row = first // held * per_owner + (z * views + v) * groups + first % held // per_row
        return jnp.where(mask, jnp.broadcast_to(wide[pl.ds(row, 1), :], (per_row, lanes)), 0.0)

    def spread_frames(z):
        for v in range(views):
            back = jnp.concatenate([line(z, v, n) for n in range(0, cells, per_row)], axis=0)
            frames[z * views + v] = dot(toft[v], back.astype(BF16), NT).astype(BF16)

    def edge_frames(n, edge):
        extra = []
        for v in range(views):
            near = [line(z, v, first) for z in range(slices) for first in (edge - 8, edge)]
            weights = jnp.concatenate([tof[v]] * per_row, axis=0)
            near = dot(jnp.concatenate(near, axis=0).astype(BF16), weights).astype(BF16).astype(F32)
            above, below = corner_columns(edge_y[v, n], cells)
            for z in range(slices):
                own = near[16 * z : 16 * z + 16]
                extra.append(sum(above[m] * own[8 + m : 9 + m] for m in range(BAND)))
                extra.append(sum(below[m] * own[7 - m : 8 - m] for m in range(BAND)))
        turned[n] = jnp.concatenate(extra, axis=0).T

    def unrotate(z):
        for v in range(views):
            i = z * views + v
            parts = [
                dot(frames[i, :, at : at + block], ryt[v, at : at + block, at : at + block])
                for at in range(0, cells, block)
            ]
            parts = add_sides(parts, [turned[n] for n in range(len(edges))], 16 * (v * slices + z))
            for n, part in enumerate(parts):
                part = part.astype(BF16)
                for w in range(cells // NARROW):
                    unrotated[z, w, v * NARROW : (v + 1) * NARROW, n * block : (n + 1) * block] = part[
                        w * NARROW : (w + 1) * NARROW
                    ]

    def finish_slice(z):
        for w in range(cells // NARROW):
            part = dot(strips_x[w], unrotated[z, w])
            first, last = part[:8], part[-8:]
            for v in range(views):
                if w > 0:
                    end = (v + 1) * NARROW
                    near = unrotated[z, w - 1, end - 16 : end, :].astype(F32)
                    for m in range(BAND):
                        first += ends_x[v][w - 1][1][m] * near[15 - m : 16 - m]
                if (w + 1) * NARROW < cells:
                    near = unrotated[z, w + 1, v * NARROW : v * NARROW + 16, :].astype(F32)
                    for m in range(BAND):
                        last += ends_x[v][w][0][m] * near[m : m + 1]
            part = jnp.concatenate([first, part[8:-8], last], axis=0)
            rows = slice(w * NARROW, (w + 1) * NARROW)
            if finish:
                part = image[z, rows, :] * part / sensitivity[z, rows, :]
            result[z, rows, :] = part
            if z == slices - 1:
                keep(result.at[z, rows], out_hbm.at[z, rows])
        if z < slices - 1:
            keep(result.at[z], out_hbm.at[z])

    def keep(source, target):
        store = pltpu.make_async_copy(source, target, sems.at[len(stores)])
        store.start()
        stores.append(store)

    spread_frames(0)
    for n, edge in enumerate(edges):
        edge_frames(n, edge)
    for z in range(slices):
        unrotate(z)
        if z + 1 < slices:
            spread_frames(z + 1)
        finish_slice(z)
    for store in stores:
        store.wait()


def local(view_size, image, sensitivity, resample_x, resample_y, tof_kernel, axial_mix, background, counts):
    views, bins, cells = tof_kernel.shape
    slices, nx, ny = image.shape
    held, planes = background.shape[2:]
    owners = planes // slices
    lanes = slices * views * bins
    vmem = pl.BlockSpec(memory_space=pltpu.VMEM)
    anywhere = pl.BlockSpec(memory_space=pl.ANY)

    block = min(BLOCK, nx)
    narrow = nx // NARROW
    wire, current, strips_x, ryt, edge_y, edge_x, toft, tof = pl.pallas_call(
        functools.partial(forward_kernel, views, slices, bins),
        in_specs=[anywhere] * 4,
        out_specs=[vmem] * 8,
        out_shape=[
            pltpu.VMEM((ny, lanes), BF16),
            pltpu.VMEM(image.shape, F32),
            pltpu.VMEM((narrow, NARROW, views * NARROW), BF16),
            pltpu.VMEM(resample_y.shape, BF16),
            pltpu.VMEM((views, max(ny // block - 1, 1), 2 * NEAR, 256), BF16),
            pltpu.VMEM((views, max(narrow - 1, 1), 2 * NEAR, 256), BF16),
            pltpu.VMEM((views, nx, lanes), BF16),
            pltpu.VMEM(tof_kernel.shape, BF16),
        ],
        scratch_shapes=[
            pltpu.VMEM(resample_x.shape, BF16),
            pltpu.VMEM(resample_y.shape, BF16),
            pltpu.VMEM((slices * views, nx, ny), BF16),
            pltpu.VMEM((slices * views, nx, ny), BF16),
            pltpu.SemaphoreType.DMA((4 * (nx // block) + slices,)),
        ],
        compiler_params=pltpu.CompilerParams(vmem_limit_bytes=VMEM_LIMIT),
        name="project",
    )(*map(in_hbm, (image, resample_x, resample_y, tof_kernel)))
    wire = lax.all_to_all(
        wire.reshape(owners, held, lanes), "slab", 0, 0, tiled=True
    ).reshape(ny, lanes)

    per_owner = slices * views * (held * bins // lanes)
    back = pl.pallas_call(
        functools.partial(middle_kernel, views, slices, bins, owners, held),
        out_specs=vmem,
        out_shape=pltpu.VMEM((owners * per_owner, lanes), BF16),
        scratch_shapes=[
            pltpu.VMEM((planes, planes), F32),
            pltpu.VMEM((owners * per_owner, lanes), F32),
            pltpu.VMEM((owners * held, lanes), F32),
        ],
        compiler_params=pltpu.CompilerParams(vmem_limit_bytes=VMEM_LIMIT),
        cost_estimate=pl.CostEstimate(flops=0, bytes_accessed=40 * 1024 * 1024, transcendentals=0),
        name="compare",
    )(
        wire,
        axial_mix,
        background.reshape(-1, planes),
        counts.reshape(-1, planes),
    )
    back = lax.all_to_all(
        back.reshape(owners, per_owner, lanes), "slab", 0, 0, tiled=True
    ).reshape(owners * per_owner, lanes)

    finish = view_size == 1
    operands = [back, tof, toft, ryt, strips_x, edge_y, edge_x]
    if finish:
        operands += [current, sensitivity]
    result = pl.pallas_call(
        functools.partial(backward_kernel, views, slices, bins, owners, held, finish),
        in_specs=[vmem] * len(operands),
        out_specs=anywhere,
        out_shape=jax.ShapeDtypeStruct((slices, nx, ny), F32),
        scratch_shapes=[
            pltpu.VMEM(image.shape, F32),
            pltpu.VMEM((owners * per_owner, lanes), F32),
            pltpu.VMEM((slices * views, nx, ny), BF16),
            pltpu.VMEM((slices, narrow, views * NARROW, ny), BF16),
            pltpu.VMEM((max(ny // block - 1, 1), nx, 16 * slices * views), F32),
            pltpu.SemaphoreType.DMA((slices - 1 + narrow,)),
        ],
        compiler_params=pltpu.CompilerParams(vmem_limit_bytes=VMEM_LIMIT),
        name="backproject",
    )(*operands)
    if finish:
        return result
    gradient = lax.psum_scatter(result, "view", scatter_dimension=1, tiled=True)
    own_rows = nx // view_size
    own = lax.dynamic_slice_in_dim(image, lax.axis_index("view") * own_rows, own_rows, 1)
    return own * gradient / sensitivity


def solution(mesh):
    in_specs = (
        P("slab", None, None),
        P("slab", "view", None),
        P("view", None, None),
        P("view", None, None),
        P("view", None, None),
        P("view", None, None),
        P("view", None, "slab", None),
        P("view", None, "slab", None),
    )
    out_specs = P("slab", "view", None)
    return jax.shard_map(
        functools.partial(local, mesh.shape["view"]),
        mesh=mesh,
        in_specs=in_specs,
        out_specs=out_specs,
        check_vma=False,
    )
```

```python
import functools

import jax
import jax.numpy as jnp
from jax import lax
from jax.experimental import pallas as pl
from jax.experimental.pallas import tpu as pltpu
from jax.sharding import PartitionSpec as P

F32, BF16 = jnp.float32, jnp.bfloat16
VMEM_LIMIT = 24 * 1024 * 1024
FIRST_LIMIT = 60 * 1024 * 1024
BLOCK, NARROW, BAND, NEAR = 256, 128, 3, 16
POWER, OFFSET = 41.5, 86.3
NN = (((1,), (0,)), ((), ()))
NT = (((1,), (1,)), ((), ()))


def dot(a, b, dims=NN):
    return lax.dot_general(a, b, dims, preferred_element_type=F32)


def halves(x):
    high = x.astype(BF16)
    return high, (x - high.astype(F32)).astype(BF16)


def dot3(a, b, dims=NN):
    ah, al = halves(a)
    bh, bl = halves(b)
    return dot(ah, bh, dims) + (dot(ah, bl, dims) + dot(al, bh, dims))


def encode(x):
    place = POWER * jnp.log(1.0 + 2.0 * x) - 2.0 * OFFSET
    size = jnp.exp(jnp.abs(place) - OFFSET)
    return jnp.where(place < 0.0, -size, size)


def decode(y):
    y = y.astype(F32)
    size = jnp.log(jnp.abs(y)) + OFFSET
    place = jnp.where(y < 0.0, -size, size)
    return 0.5 * jnp.exp((place + 2.0 * OFFSET) * (1.0 / POWER)) - 0.5


def in_hbm(x):
    return pltpu.with_memory_space_constraint(x, pltpu.HBM)


def forward_kernel(
    views, slices, bins, image_hbm, rx_hbm, ry_hbm, tof_hbm,
    out, image, strips_x, ryt, edge_y, edge_x, toft, tof, rx, ry, along, rotated, sems,
):
    cells = rx.shape[1]
    block = min(BLOCK, cells)

    def band(source, target, edge, step):
        copies = []
        for at in range(0, cells, block):
            place = (slice(None), pl.ds(at, block), pl.ds(at, block))
            copies.append((source.at[place], target.at[place]))
            if at > 0:
                window = (slice(None), pl.ds(at - NEAR, 2 * NEAR), pl.ds(at - 128, 256))
                copies.append((source.at[window], edge.at[:, at // step - 1]))
        return copies

    images = [(image_hbm.at[z], image.at[z]) for z in range(slices)]
    top, bottom = pl.ds(0, block), pl.ds(block, cells - block)
    groups = [band(ry_hbm, ry, edge_y, block) + [(image_hbm.at[0, top], image.at[0, top])]]
    groups += [[(image_hbm.at[0, bottom], image.at[0, bottom])]]
    groups += [images[1:2], [(tof_hbm, tof)] + band(rx_hbm, rx, edge_x, NARROW)]
    groups += [[pair] for pair in images[2:]]
    loads, n = [], 0
    for group in groups:
        loads.append([pltpu.make_async_copy(*pair, sems.at[n + i]) for i, pair in enumerate(group)])
        n += len(group)
    for load in sum(loads, []):
        load.start()
    loads = iter(loads)

    def arrive():
        for load in next(loads):
            load.wait()

    per_row = toft.shape[2] // bins
    edges = range(block, cells, block)
    coded = []

    def along_second(z, rows=slice(None)):
        low = image[z, rows].astype(BF16)
        extra = [dot(low[:, e - 128 : e + 128], corners[n]) for n, e in enumerate(edges)]
        for v in range(views):
            parts = [
                dot(low[:, at : at + block], ry[v, at : at + block, at : at + block])
                for at in range(0, cells, block)
            ]
            parts = add_sides(parts, extra, 16 * v)
            for n, part in enumerate(parts):
                along[z * views + v, rows, n * block : (n + 1) * block] = part.astype(BF16)

    def along_first(z):
        for v in range(views):
            i = z * views + v
            parts = [
                dot(rx[v, at : at + block, at : at + block], along[i, at : at + block, :])
                for at in range(0, cells, block)
            ]
            for n, e in enumerate(edges):
                above, below = sides[v][n]
                near = along[i, e - 16 : e + 16, :].astype(F32)
                last, first = parts[n][-8:], parts[n + 1][:8]
                for m in range(BAND):
                    last += above[m] * near[16 + m : 17 + m]
                    first += below[m] * near[15 - m : 16 - m]
                parts[n] = jnp.concatenate([parts[n][:-8], last], axis=0)
                parts[n + 1] = jnp.concatenate([first, parts[n + 1][8:]], axis=0)
            for n, part in enumerate(parts):
                rotated[i, n * block : (n + 1) * block, :] = part.astype(BF16)

    def along_rays(z):
        for v in range(views):
            coded.append(encode(dot(tof[v], rotated[z * views + v])))

    arrive()
    corners = []
    for n in range(len(edges)):
        near = [corner(edge_y[v, n])[:, 120:136] for v in range(views)]
        near = jnp.concatenate(near + [jnp.zeros((2 * NEAR, 128 - 16 * views), F32)], axis=1)
        above = jnp.zeros((128 - NEAR, 128), F32)
        corners.append(jnp.concatenate([above, near, above], axis=0).astype(BF16))
    along_second(0, slice(0, block))
    arrive()
    along_second(0, slice(block, cells))
    between = block // NARROW
    for z in range(1, slices):
        arrive()
        along_second(z)
        if z == 1:
            arrive()
            sides = [
                [corner_columns(edge_x[v, (n + 1) * between - 1], cells) for n in range(len(edges))]
                for v in range(views)
            ]
        along_first(z - 1)
        if z > 1:
            along_rays(z - 2)
        if z == 1:
            for v in range(views):
                for n, at in enumerate(range(0, cells, NARROW)):
                    strips_x[n, :, v * NARROW : (v + 1) * NARROW] = rx[
                        v, at : at + NARROW, at : at + NARROW
                    ].T
                    if at % block > 0:
                        edge_x[v, n - 1] = rx[v, at - NEAR : at + NEAR, at - 128 : at + 128]
        if z == min(2, slices - 1):
            for v in range(views):
                toft[v] = jnp.concatenate([tof[v]] * per_row, axis=0).T
                for at in range(0, cells, block):
                    here = slice(at, at + block)
                    ryt[v, here, here] = ry[v, here, here].T
    along_rays(slices - 2)
    along_first(slices - 1)
    along_rays(slices - 1)
    out[...] = jnp.concatenate(coded, axis=0).T.astype(BF16)


def add_sides(parts, extra, spot):
    parts = list(parts)
    for n, columns in enumerate(extra):
        lane = lax.broadcasted_iota(jnp.int32, columns.shape, 1)
        columns = pltpu.roll(columns, (120 - spot) % 128, 1)
        left, right = parts[n], parts[n + 1]
        parts[n] = jnp.concatenate(
            [left[:, :-128], left[:, -128:] + jnp.where(lane >= 120, columns, 0.0)], axis=1
        )
        parts[n + 1] = jnp.concatenate(
            [right[:, :128] + jnp.where(lane < 8, columns, 0.0), right[:, 128:]], axis=1
        )
    return parts


def swap_blocks(parts, width):
    n = len(parts)
    lane = lax.broadcasted_iota(jnp.int32, parts[0].shape, 1) // width
    step = 1
    while step < n:
        low = (lane // step) % 2 == 0
        new = list(parts)
        for i in range(n):
            if (i // step) % 2 == 0:
                a, b = parts[i], parts[i + step]
                shift = step * width
                new[i] = jnp.where(low, a, pltpu.roll(b, shift, 1))
                new[i + step] = jnp.where(
                    low, pltpu.roll(a, a.shape[1] - shift, 1), b
                )
        parts = new
        step *= 2
    return parts


def middle_kernel(views, slices, bins, owners, held, wire, mix, background, counts, out, turned, spread, sums_in):
    rows = views * bins
    lanes = slices * rows
    sums_in[...] = decode(wire[...])
    blocks = []
    for first in range(0, held, slices):
        parts = [
            sums_in[pl.ds(first + i, owners, stride=held), :] for i in range(slices)
        ]
        blocks.append(jnp.concatenate(swap_blocks(parts, rows), axis=0).T)
    for v in range(views):
        turned[...] = mix[v].T
        mixed = jnp.concatenate(
            [turned[pl.ds(s, owners, stride=slices), :] for s in range(slices)], axis=0
        )
        sums = jnp.concatenate(
            [
                blocks[j // slices][
                    (j % slices) * rows + v * bins : (j % slices) * rows + (v + 1) * bins
                ]
                for j in range(held)
            ],
            axis=0,
        )
        base = v * bins * held
        added = jnp.concatenate(
            [background[pl.ds(base + j, bins, stride=held), :] for j in range(held)], axis=0
        )
        seen = jnp.concatenate(
            [counts[pl.ds(base + j, bins, stride=held), :] for j in range(held)], axis=0
        )
        ratios = seen.astype(F32) / (added + dot3(sums, mixed))
        back = dot3(mixed, ratios, NT)
        groups = held * bins // lanes
        for s in range(slices):
            for g in range(groups):
                spread[pl.ds((s * views + v) * groups + g, owners, stride=slices * views * groups), :] = back[
                    s * owners : (s + 1) * owners, g * lanes : (g + 1) * lanes
                ]
    out[...] = spread[...].astype(BF16)


def corner(window):
    window = window.astype(F32)
    row = lax.broadcasted_iota(jnp.int32, window.shape, 0) < window.shape[0] // 2
    column = lax.broadcasted_iota(jnp.int32, window.shape, 1) < window.shape[1] // 2
    return jnp.where(row != column, window, 0.0)


def corner_columns(window, width):
    near = corner(window)[NEAR - 8 : NEAR + 8]
    spread = lambda rows, n: jnp.broadcast_to(near[rows, n : n + 1], (8, width))
    return (
        [spread(slice(0, 8), 128 + n) for n in range(BAND)],
        [spread(slice(8, 16), 127 - n) for n in range(BAND)],
    )


def corner_rows(window, width):
    near = corner(window)[:, 120:136]
    flat = jnp.concatenate([near, jnp.zeros((2 * NEAR, 112), F32)], axis=1)
    turned = jnp.concatenate([flat, jnp.zeros((128 - 2 * NEAR, 128), F32)], axis=0).T
    spread = lambda rows, n: jnp.broadcast_to(turned[rows, n : n + 1], (8, width))
    return (
        [spread(slice(0, 8), NEAR + n) for n in range(BAND)],
        [spread(slice(8, 16), NEAR - 1 - n) for n in range(BAND)],
    )


def backward_kernel(views, slices, bins, owners, held, finish, *refs):
    wire, tof, toft, ryt, strips_x, edge_y, edge_x = refs[:7]
    if finish:
        image, sensitivity = refs[7:9]
    out_hbm, result, wide, frames, unrotated, turned, sems = refs[-7:]

    cells = ryt.shape[1]
    lanes = wire.shape[1]
    per_row = lanes // bins
    groups = held // per_row
    per_owner = slices * views * groups
    wide[...] = wire[...].astype(F32)
    mask = (
        lax.broadcasted_iota(jnp.int32, (per_row, lanes), 1) // bins
        == lax.broadcasted_iota(jnp.int32, (per_row, lanes), 0)
    )
    block = min(BLOCK, cells)
    edges = range(block, cells, block)
    narrow_edges = range(NARROW, cells, NARROW)
    ends_x = [[corner_rows(edge_x[v, n], cells) for n in range(len(narrow_edges))] for v in range(views)]
    stores = []

    def line(z, v, first):
        row = first // held * per_owner + (z * views + v) * groups + first % held // per_row
        return jnp.where(mask, jnp.broadcast_to(wide[pl.ds(row, 1), :], (per_row, lanes)), 0.0)

    def spread_frames(z):
        for v in range(views):
            back = jnp.concatenate([line(z, v, n) for n in range(0, cells, per_row)], axis=0)
            frames[z * views + v] = dot(toft[v], back.astype(BF16), NT).astype(BF16)

    def edge_frames(n, edge):
        extra = []
        for v in range(views):
            near = [line(z, v, first) for z in range(slices) for first in (edge - 8, edge)]
            weights = jnp.concatenate([tof[v]] * per_row, axis=0)
            near = dot(jnp.concatenate(near, axis=0).astype(BF16), weights).astype(BF16).astype(F32)
            above, below = corner_columns(edge_y[v, n], cells)
            for z in range(slices):
                own = near[16 * z : 16 * z + 16]
                extra.append(sum(above[m] * own[8 + m : 9 + m] for m in range(BAND)))
                extra.append(sum(below[m] * own[7 - m : 8 - m] for m in range(BAND)))
        turned[n] = jnp.concatenate(extra, axis=0).T

    def unrotate(z):
        for v in range(views):
            i = z * views + v
            parts = [
                dot(frames[i, :, at : at + block], ryt[v, at : at + block, at : at + block])
                for at in range(0, cells, block)
            ]
            parts = add_sides(parts, [turned[n] for n in range(len(edges))], 16 * (v * slices + z))
            for n, part in enumerate(parts):
                part = part.astype(BF16)
                for w in range(cells // NARROW):
                    unrotated[z, w, v * NARROW : (v + 1) * NARROW, n * block : (n + 1) * block] = part[
                        w * NARROW : (w + 1) * NARROW
                    ]

    def finish_slice(z):
        for w in range(cells // NARROW):
            part = dot(strips_x[w], unrotated[z, w])
            first, last = part[:8], part[-8:]
            for v in range(views):
                if w > 0:
                    end = (v + 1) * NARROW
                    near = unrotated[z, w - 1, end - 16 : end, :].astype(F32)
                    for m in range(BAND):
                        first += ends_x[v][w - 1][1][m] * near[15 - m : 16 - m]
                if (w + 1) * NARROW < cells:
                    near = unrotated[z, w + 1, v * NARROW : v * NARROW + 16, :].astype(F32)
                    for m in range(BAND):
                        last += ends_x[v][w][0][m] * near[m : m + 1]
            part = jnp.concatenate([first, part[8:-8], last], axis=0)
            rows = slice(w * NARROW, (w + 1) * NARROW)
            if finish:
                part = image[z, rows, :] * part / sensitivity[z, rows, :]
            result[z, rows, :] = part
            if z == slices - 1:
                keep(result.at[z, rows], out_hbm.at[z, rows])
        if z < slices - 1:
            keep(result.at[z], out_hbm.at[z])

    def keep(source, target):
        store = pltpu.make_async_copy(source, target, sems.at[len(stores)])
        store.start()
        stores.append(store)

    spread_frames(0)
    for n, edge in enumerate(edges):
        edge_frames(n, edge)
    for z in range(slices):
        unrotate(z)
        if z + 1 < slices:
            spread_frames(z + 1)
        finish_slice(z)
    for store in stores:
        store.wait()


def local(view_size, image, sensitivity, resample_x, resample_y, tof_kernel, axial_mix, background, counts):
    views, bins, cells = tof_kernel.shape
    slices, nx, ny = image.shape
    held, planes = background.shape[2:]
    owners = planes // slices
    lanes = slices * views * bins
    vmem = pl.BlockSpec(memory_space=pltpu.VMEM)
    anywhere = pl.BlockSpec(memory_space=pl.ANY)

    block = min(BLOCK, nx)
    narrow = nx // NARROW
    wire, current, strips_x, ryt, edge_y, edge_x, toft, tof = pl.pallas_call(
        functools.partial(forward_kernel, views, slices, bins),
        in_specs=[anywhere] * 4,
        out_specs=[vmem] * 8,
        out_shape=[
            pltpu.VMEM((ny, lanes), BF16),
            pltpu.VMEM(image.shape, F32),
            pltpu.VMEM((narrow, NARROW, views * NARROW), BF16),
            pltpu.VMEM(resample_y.shape, BF16),
            pltpu.VMEM((views, max(ny // block - 1, 1), 2 * NEAR, 256), BF16),
            pltpu.VMEM((views, max(narrow - 1, 1), 2 * NEAR, 256), BF16),
            pltpu.VMEM((views, nx, lanes), BF16),
            pltpu.VMEM(tof_kernel.shape, BF16),
        ],
        scratch_shapes=[
            pltpu.VMEM(resample_x.shape, BF16),
            pltpu.VMEM(resample_y.shape, BF16),
            pltpu.VMEM((slices * views, nx, ny), BF16),
            pltpu.VMEM((slices * views, nx, ny), BF16),
            pltpu.SemaphoreType.DMA((4 * (nx // block) + slices,)),
        ],
        compiler_params=pltpu.CompilerParams(vmem_limit_bytes=VMEM_LIMIT),
        name="project",
    )(*map(in_hbm, (image, resample_x, resample_y, tof_kernel)))
    wire = lax.all_to_all(
        wire.reshape(owners, held, lanes), "slab", 0, 0, tiled=True
    ).reshape(ny, lanes)

    per_owner = slices * views * (held * bins // lanes)
    back = pl.pallas_call(
        functools.partial(middle_kernel, views, slices, bins, owners, held),
        out_specs=vmem,
        out_shape=pltpu.VMEM((owners * per_owner, lanes), BF16),
        scratch_shapes=[
            pltpu.VMEM((planes, planes), F32),
            pltpu.VMEM((owners * per_owner, lanes), F32),
            pltpu.VMEM((owners * held, lanes), F32),
        ],
        compiler_params=pltpu.CompilerParams(vmem_limit_bytes=VMEM_LIMIT),
        cost_estimate=pl.CostEstimate(flops=0, bytes_accessed=40 * 1024 * 1024, transcendentals=0),
        name="compare",
    )(
        wire,
        axial_mix,
        background.reshape(-1, planes),
        counts.reshape(-1, planes),
    )
    back = lax.all_to_all(
        back.reshape(owners, per_owner, lanes), "slab", 0, 0, tiled=True
    ).reshape(owners * per_owner, lanes)

    finish = view_size == 1
    operands = [back, tof, toft, ryt, strips_x, edge_y, edge_x]
    if finish:
        operands += [current, sensitivity]
    result = pl.pallas_call(
        functools.partial(backward_kernel, views, slices, bins, owners, held, finish),
        in_specs=[vmem] * len(operands),
        out_specs=anywhere,
        out_shape=jax.ShapeDtypeStruct((slices, nx, ny), F32),
        scratch_shapes=[
            pltpu.VMEM(image.shape, F32),
            pltpu.VMEM((owners * per_owner, lanes), F32),
            pltpu.VMEM((slices * views, nx, ny), BF16),
            pltpu.VMEM((slices, narrow, views * NARROW, ny), BF16),
            pltpu.VMEM((max(ny // block - 1, 1), nx, 16 * slices * views), F32),
            pltpu.SemaphoreType.DMA((slices - 1 + narrow,)),
        ],
        compiler_params=pltpu.CompilerParams(vmem_limit_bytes=VMEM_LIMIT),
        name="backproject",
    )(*operands)
    if finish:
        return result
    gradient = lax.psum_scatter(result, "view", scatter_dimension=1, tiled=True)
    own_rows = nx // view_size
    own = lax.dynamic_slice_in_dim(image, lax.axis_index("view") * own_rows, own_rows, 1)
    return own * gradient / sensitivity


def solution(mesh):
    in_specs = (
        P("slab", None, None),
        P("slab", "view", None),
        P("view", None, None),
        P("view", None, None),
        P("view", None, None),
        P("view", None, None),
        P("view", None, "slab", None),
        P("view", None, "slab", None),
    )
    out_specs = P("slab", "view", None)
    return jax.shard_map(
        functools.partial(local, mesh.shape["view"]),
        mesh=mesh,
        in_specs=in_specs,
        out_specs=out_specs,
        check_vma=False,
    )
```
